128 devices in a mesh: seq: 8 (over y, z_lo), head: 16 (over z_hi, x, core).
Axes of the slice: x: 4, y: 4, z: 4 (z_hi: 2, z_lo: 2; z = z_hi * 2 + z_lo), core: 2. Of those that a mesh axis runs over, the one named last changes fastest.
Arguments:
- inner_x: bfloat16 [8192, 16384], P('seq', 'head'), may hold values from -6 to 6
- gate_z: bfloat16 [8192, 16384], P('seq', 'head'), may hold values from -6 to 6
- dt_raw: bfloat16 [256, 8192], P('head', 'seq'), may hold values from -4.7 to 4.7
- b_proj: bfloat16 [8192, 2048], P(('seq', 'head')), may hold values from -3 to 3
- c_proj: bfloat16 [8192, 2048], P(('seq', 'head')), may hold values from -0.375 to 0.375
- a_log: float32 [256], P('head'), may hold values from -12 to 0
- dt_bias: float32 [256], P('head'), may hold values from -4 to -3
- d_skip: float32 [256], P('head'), may hold values from 0.5 to 2
- grad_gated: bfloat16 [8192, 16384], P('seq', 'head'), may hold values from -16 to 16
Outputs:
- gated: bfloat16 [8192, 16384], P('seq', 'head')
- grad_x: bfloat16 [8192, 16384], P('seq', 'head')
- grad_z: bfloat16 [8192, 16384], P('seq', 'head')
- grad_dt: bfloat16 [256, 8192], P('head', 'seq')
- grad_b: bfloat16 [8192, 2048], P(('seq', 'head'))
- grad_c: bfloat16 [8192, 2048], P(('seq', 'head'))
- grad_alog: float32 [256], P('head')
- grad_bias: float32 [256], P('head')
- grad_skip: float32 [256], P('head')
The draws below stay inside these ranges and needn't reach their ends.
All inputs are finite; a program needn't handle non-finite values.
Results may differ from the reference program's by a relative error of at most 0.014.
Values may be sent and summed in bfloat16 or wider, within the bound.
A program may use at most 256 MiB of HBM per device.

```python
import math
import jax
import jax.numpy as jnp
from jax import lax

NHEADS = 256
HEAD_DIM = 64
STATE = 256
GROUPS = 8
STRETCH = 128
TOK_DEV = 1024
TOKENS = 8192


def draw_dt_raw(key, part):
    key = jax.random.fold_in(key, 11)
    key_base, key_offset = jax.random.split(key)
    blocks = TOKENS // STRETCH
    offsets = jax.random.uniform(key_offset, (NHEADS, blocks, 1), jnp.float32, -0.7, 0.7)
    base = jnp.clip(jax.random.normal(key_base, (NHEADS, blocks, STRETCH), jnp.float32), -4.0, 4.0)
    return (base + offsets).reshape(NHEADS, TOKENS).astype(jnp.bfloat16)


def draw_a_log(key, part):
    key = jax.random.fold_in(key, 23)
    key_pick, key_slow, key_fast, key_middle = jax.random.split(key, 4)
    picks = jax.random.uniform(key_pick, (NHEADS,), jnp.float32)
    slow_rate = jnp.exp(jax.random.uniform(key_slow, (NHEADS,), jnp.float32, math.log(0.05), math.log(0.6))) / TOKENS
    fast_rate = jax.random.uniform(key_fast, (NHEADS,), jnp.float32, 1.0 / 50.0, 1.0 / 30.0)
    middle_reach = jnp.exp(jax.random.uniform(key_middle, (NHEADS,), jnp.float32, math.log(1.0), math.log(6.0)))
    middle_rate = jnp.minimum(middle_reach / TOK_DEV, 1.0 / 30.0)
    slow_share = 0.5
    middle_share = 0.3
    rates = jnp.where(picks < slow_share, slow_rate, jnp.where(picks < slow_share + middle_share, middle_rate, fast_rate))
    return jnp.log(rates / 0.05)


def draw_grad_gated(key, part):
    key = jax.random.fold_in(key, 37)
    position = jnp.arange(TOKENS, dtype=jnp.float32)[:, None] / TOKENS
    shape = (TOKENS, NHEADS * HEAD_DIM)
    base = jnp.clip(jax.random.normal(key, shape, jnp.float32), -4.0, 4.0)
    rising = 1.0 + 2.0 * position
    return (base * rising).astype(jnp.bfloat16)


def level_of(rng, extent, cuts, low, top_value):
    level = 1.0
    for dim, shards_of in cuts:
        draws = jax.random.uniform(jax.random.fold_in(jax.random.fold_in(rng, 6), dim), (shards_of,), jnp.float32, low / len(cuts), top_value / len(cuts))
        level = level * jnp.repeat(jnp.exp(draws), extent[dim] // shards_of).reshape((-1,) + (1,) * (len(extent) - 1 - dim))
    return level


def bell_draw(stream_key, dims, deviation, bound, shards=(), kind=jnp.bfloat16):
    level = level_of(stream_key, dims, shards, -0.22, 0.18) if shards else 1.0
    drawn = jax.random.normal(stream_key, dims, jnp.float32) * deviation * level
    return jnp.minimum(jnp.maximum(drawn, -bound), bound).astype(kind)


def setup_inputs(seed: int = 0) -> dict:
    streams_of = jax.random.split(jax.random.key(seed), 10)
    return {
        "inner_x": bell_draw(streams_of[0], (TOKENS, NHEADS * HEAD_DIM), 1.0, 6.0, ((0, 8), (1, 16))),
        "gate_z": bell_draw(streams_of[1], (TOKENS, NHEADS * HEAD_DIM), 1.0, 6.0, ((0, 8), (1, 16))),
        "dt_raw": draw_dt_raw(jax.random.fold_in(streams_of[9], 71), 0),
        "b_proj": bell_draw(streams_of[3], (TOKENS, GROUPS * STATE), 0.5, 3.0, ((0, 128),)),
        "c_proj": bell_draw(streams_of[4], (TOKENS, GROUPS * STATE), STATE ** -0.5, 0.375, ((0, 128),)),
        "a_log": draw_a_log(jax.random.fold_in(streams_of[9], 71), 0),
        "dt_bias": jnp.clip(-4.0 + 1.0 * jax.random.uniform(streams_of[6], (NHEADS,), jnp.float32) ** level_of(streams_of[6], (NHEADS,), ((0, 16),), -0.2, 0.2), -4.0, -3.0),
        "d_skip": jnp.clip(0.5 + 1.5 * jax.random.uniform(streams_of[7], (NHEADS,), jnp.float32) ** level_of(streams_of[7], (NHEADS,), ((0, 16),), -0.2, 0.2), 0.5, 2.0),
        "grad_gated": draw_grad_gated(jax.random.fold_in(streams_of[9], 71), 0),
    }


highest = lax.Precision.HIGHEST

def stretch_scan(values, steps, decays, b_rows, c_rows, start_state):
    cum_decay = jnp.cumsum(decays, axis=2)
    positions = jnp.arange(values.shape[1])
    lower_mask = positions[:, None] >= positions[None, :]
    segments = cum_decay[:, :, :, None] - cum_decay[:, :, None, :]
    decay_mask = jnp.exp(jnp.where(lower_mask, segments, -jnp.inf))
    scores = jnp.einsum('cin,cjn->cij', c_rows, b_rows, precision=highest)
    mixing = scores[None] * decay_mask * steps[:, :, None, :]
    y_diag = jnp.einsum('kcij,cjkp->cikp', mixing, values, precision=highest)
    last_decay = cum_decay[:, :, -1:]
    weights = jnp.exp(last_decay - cum_decay) * steps
    scaled = values * jnp.transpose(weights, (1, 2, 0))[..., None]
    states = jnp.einsum('cjn,cjkp->cknp', b_rows, scaled, precision=highest)
    totals = jnp.transpose(last_decay[:, :, 0])

    def advance(state_now, inputs):
        total_step, local_state = inputs
        return (jnp.exp(total_step)[:, None, None] * state_now + local_state, state_now)
    final_state, starts = lax.scan(advance, start_state, (totals, states))
    y_off = jnp.einsum('cin,cknp->cikp', c_rows, starts, precision=highest)
    y_off = y_off * jnp.transpose(jnp.exp(cum_decay), (1, 2, 0))[..., None]
    return (y_diag + y_off, final_state)

def mixer_local(inner_x, gate_z, dt_raw, b_group, c_group, a_log, dt_bias, d_skip, start_state):
    token_count = inner_x.shape[0]
    head_count = a_log.shape[0]
    blocks = token_count // STRETCH
    step_size = jax.nn.softplus(dt_raw.astype(jnp.float32) + dt_bias[:, None])
    log_decay = -jnp.exp(a_log)[:, None] * step_size
    values = inner_x.astype(jnp.float32).reshape(blocks, STRETCH, head_count, HEAD_DIM)
    y_core, final_state = stretch_scan(values, step_size.reshape(head_count, blocks, STRETCH), log_decay.reshape(head_count, blocks, STRETCH), b_group.reshape(blocks, STRETCH, STATE), c_group.reshape(blocks, STRETCH, STATE), start_state)
    y_full = y_core + d_skip[None, None, :, None] * values
    y_full = y_full.reshape(token_count, head_count * HEAD_DIM)
    return (y_full * jax.nn.silu(gate_z.astype(jnp.float32)), final_state)

def mixer_all(inner_x, gate_z, dt_raw, b_proj, c_proj, a_log, dt_bias, d_skip):
    heads_group = NHEADS // GROUPS
    x_groups = jnp.transpose(inner_x.reshape(TOKENS, GROUPS, heads_group * HEAD_DIM), (1, 0, 2))
    z_groups = jnp.transpose(gate_z.reshape(TOKENS, GROUPS, heads_group * HEAD_DIM), (1, 0, 2))
    dt_groups = dt_raw.reshape(GROUPS, heads_group, TOKENS)
    b_groups = jnp.transpose(b_proj.reshape(TOKENS, GROUPS, STATE), (1, 0, 2))
    c_groups = jnp.transpose(c_proj.reshape(TOKENS, GROUPS, STATE), (1, 0, 2))
    alog_groups = a_log.reshape(GROUPS, heads_group)
    bias_groups = dt_bias.reshape(GROUPS, heads_group)
    skip_groups = d_skip.reshape(GROUPS, heads_group)

    def one_group(inputs):
        x_one, z_one, dt_one, b_one, c_one, alog_one, bias_one, skip_one = inputs
        empty_state = jnp.zeros((heads_group, STATE, HEAD_DIM), jnp.float32)
        result, final_state = mixer_local(x_one, z_one, dt_one, b_one.astype(jnp.float32), c_one.astype(jnp.float32), alog_one, bias_one, skip_one, empty_state)
        return result
    outputs = lax.map(jax.checkpoint(one_group), (x_groups, z_groups, dt_groups, b_groups, c_groups, alog_groups, bias_groups, skip_groups))
    return jnp.transpose(outputs, (1, 0, 2)).reshape(TOKENS, NHEADS * HEAD_DIM)

def reference(inner_x, gate_z, dt_raw, b_proj, c_proj, a_log, dt_bias, d_skip, grad_gated):
    result, pullback = jax.vjp(mixer_all, inner_x, gate_z, dt_raw, b_proj, c_proj, a_log, dt_bias, d_skip)
    grads = pullback(grad_gated.astype(jnp.float32))
    return (result.astype(jnp.bfloat16), grads[0], grads[1], grads[2], grads[3], grads[4], grads[5], grads[6], grads[7])
```

```python
import jax
import jax.numpy as jnp
from jax import lax
from jax.experimental import pallas as pl
from jax.experimental.pallas import tpu as pltpu
from jax.sharding import PartitionSpec as P

HEAD_DIM = 64
STATE = 256
GROUPS = 8
L = 128
NC = 8
H = 16
W = H * HEAD_DIM
ROWS = 64
F32, BF = jnp.float32, jnp.bfloat16
MESH = pl.DeviceIdType.MESH
HIGHEST = lax.Precision.HIGHEST
LOG2E = 1.4426950408889634


def dot(a, b, ca, cb, precision=None):
    return lax.dot_general(
        a, b, (((ca,), (cb,)), ((), ())), preferred_element_type=F32, precision=precision
    )


def nn(a, b):
    return dot(a, b, 1, 0)


def nt(a, b):
    return dot(a, b, 1, 1)


def tn(a, b):
    return dot(a, b, 0, 0)


def remote(src, dst, send_sem, recv_sem, device):
    return pltpu.make_async_remote_copy(
        src_ref=src,
        dst_ref=dst,
        send_sem=send_sem,
        recv_sem=recv_sem,
        device_id=device,
        device_id_type=MESH,
    )


def rows_of(index, count):
    return pl.ds(pl.multiple_of(index * count, count), count)


def kernel(
    x_hbm, z_hbm, g_hbm, dt_ref, b_hbm, c_hbm, alog_ref, bias_ref, skip_ref,
    gated_hbm, gx_hbm, gz_hbm, gdt_ref, gb_hbm, gc_hbm, galog_ref, gbias_ref, gskip_ref,
    x_v, z_v, g_v, xp, dy, xw, dyw, dtw, ecw, ww, e_s, dtv, ecv, wv, cumv, cumt,
    elw, prew, postw, skw, bc_v, s_loc, ds_loc, s_acc, yd, dxd, stage, sib, fin, gbc,
    sendf, sendg, recvf, recvg, outf, outg, s_in, ds_in, skipacc, fw, qs, ps, par,
    in_sem, out_sem, loc_sem, a_send, a_recv, f_send, f_recv, xf_send, xf_recv, xg_send, xg_recv,
    rf_send, rf_recv, rg_send, rg_recv, sib_send, sib_recv, fin_send, fin_recv, par_send, par_recv,
    gout_sem,
):
    seq = lax.axis_index("seq")
    hd = lax.axis_index("head")
    core = lax.rem(hd, 2)
    chip = lax.div(hd, 2)
    sibling = (seq, 2 * chip + 1 - core)

    def chip_at(k):
        return lax.rem(chip + k, NC)

    def chip_dev(k):
        return (seq, 2 * chip_at(k) + core)

    def slab_at(k):
        return lax.rem(seq + k, NC)

    def slab_dev(k):
        return (slab_at(k), hd)

    def load(a, c):
        src, dst = ((x_hbm, x_v), (z_hbm, z_v), (g_hbm, g_v))[a]
        return pltpu.make_async_copy(
            src.at[rows_of(c, L)], dst.at[rows_of(c, L)], in_sem.at[a, c]
        )

    def own_bc(t):
        src = (b_hbm, c_hbm)[t]
        return pltpu.make_async_copy(
            src.at[:, rows_of(chip, STATE)], bc_v.at[t, rows_of(hd, ROWS)], loc_sem.at[t]
        )

    for c in range(NC):
        for a in range(3):
            load(a, c).start()
    for t in range(2):
        own_bc(t).start()

    barrier = pltpu.get_barrier_semaphore()
    for k in range(1, NC):
        pl.semaphore_signal(barrier, inc=1, device_id=chip_dev(k), device_id_type=MESH)
        pl.semaphore_signal(barrier, inc=1, device_id=slab_dev(k), device_id_type=MESH)
    pl.semaphore_signal(barrier, inc=1, device_id=sibling, device_id_type=MESH)
    pl.semaphore_wait(barrier, 2 * NC - 1)

    def spread(t, k):
        src = (b_hbm, c_hbm)[t]
        device = sibling if k == 0 else chip_dev(k)
        group = chip if k == 0 else chip_at(k)
        return remote(
            src.at[:, rows_of(group, STATE)],
            bc_v.at[t, rows_of(hd, ROWS)],
            a_send.at[t, k],
            a_recv.at[t, k],
            device,
        )

    def arrived(t, k):
        place = 2 * chip + 1 - core if k == 0 else 2 * lax.rem(chip + NC - k, NC) + core
        return remote(
            b_hbm.at[:, rows_of(chip, STATE)],
            bc_v.at[t, rows_of(place, ROWS)],
            a_send.at[t, k],
            a_recv.at[t, k],
            sibling,
        )

    def forward(k, mine):
        place = 2 * lax.rem(chip + NC - k, NC) + (core if mine else 1 - core)
        block = bc_v.at[:, rows_of(place, ROWS)]
        return remote(block, block, f_send.at[k], f_recv.at[k], sibling)

    for k in list(range(1, NC)) + [0]:
        for t in range(2):
            spread(t, k).start()

    row16 = lax.broadcasted_iota(jnp.int32, (H, L), 0)

    def per_head(ref):
        column = jnp.zeros((H, L), F32)
        for h in range(H):
            column = jnp.where(row16 == h, ref[h], column)
        return jnp.concatenate([column] * NC, axis=0)

    rate = -jnp.exp(per_head(alog_ref))
    raw = dt_ref[...].astype(F32)
    pre = jnp.concatenate([raw[:, L * c : L * c + L] for c in range(NC)], axis=0) + per_head(bias_ref)
    step = jnp.maximum(pre, 0.0) + jnp.log1p(jnp.exp(-jnp.abs(pre)))
    decay = rate * step
    iota0 = lax.broadcasted_iota(jnp.int32, (L, L), 0)
    iota1 = lax.broadcasted_iota(jnp.int32, (L, L), 1)
    upper = (iota0 <= iota1).astype(F32)
    cum = dot(decay, upper, 1, 0, HIGHEST)
    step_r = step.astype(BF)
    ecum = jnp.exp(cum)
    tail = jnp.exp(cum[:, L - 1 : L] - cum)
    cum2 = cum * LOG2E
    cum_t = jnp.transpose(cum2)
    step_t = jnp.transpose(step_r.astype(F32))
    ecum_t = jnp.transpose(ecum)
    tail_t = jnp.transpose(tail)
    for c in range(NC):
        cumv[c] = cum2[H * c : H * c + H]
        cumt[c] = cum_t[:, H * c : H * c + H]
        dtv[c] = step_t[:, H * c : H * c + H].astype(BF)
        ecv[c] = ecum_t[:, H * c : H * c + H].astype(BF)
        wv[c] = tail_t[:, H * c : H * c + H].astype(BF)
    head_of = lax.shift_right_logical(lax.broadcasted_iota(jnp.int32, (H, W), 1), 6)
    onehot = head_of == lax.broadcasted_iota(jnp.int32, (H, W), 0)
    e_s[...] = onehot.astype(BF)
    spread_f = onehot.astype(F32)
    last8 = jnp.concatenate([ecum_t[L - 1 : L, H * c : H * c + H] for c in range(NC)], axis=0)
    elast = dot(last8, spread_f, 1, 0, HIGHEST)
    skip_row = jnp.zeros((1, W), F32)
    for h in range(H):
        skip_row = jnp.where(head_of[0:1] == h, skip_ref[h], skip_row)
    skw[...] = skip_row
    run = jnp.ones((1, W), F32)
    for c in range(NC):
        elw[c] = elast[c : c + 1]
        prew[c] = run
        run = run * elast[c : c + 1]
    slab_decay = run
    run = jnp.ones((1, W), F32)
    for c in reversed(range(NC)):
        postw[c + 1] = run
        run = run * elast[c : c + 1]
    postw[0] = run
    skipacc[...] = jnp.zeros_like(skipacc)

    def prepare(c):
        for a in range(3):
            load(a, c).wait()
        r = rows_of(c, L)
        dt_c, ec_c, w_c = dtv[c], ecv[c], wv[c]
        for p in range(W // 256):
            col = slice(256 * p, 256 * p + 256)
            e_c = e_s[:, col]
            dt_w, ec_w, w_w = nn(dt_c, e_c), nn(ec_c, e_c), nn(w_c, e_c)
            dtw[r, col] = dt_w.astype(BF)
            ecw[r, col] = ec_w.astype(BF)
            ww[r, col] = w_w.astype(BF)
            x_r = (x_v[r, col].astype(F32) * dt_w).astype(BF)
            xp[r, col] = x_r
            xw[r, col] = (x_r.astype(F32) * w_w).astype(BF)
            z = z_v[r, col].astype(F32)
            dy_r = (g_v[r, col].astype(F32) * (z / (1.0 + jnp.exp(-z)))).astype(BF)
            dy[r, col] = dy_r
            dyw[r, col] = (dy_r.astype(F32) * ec_w).astype(BF)

    def prepare_step(c, carry):
        prepare(c)
        return carry

    lax.fori_loop(0, NC, prepare_step, 0)
    for k in range(1, NC):
        for t in range(2):
            arrived(t, k).wait_recv()
        forward(k, True).start()
    for t in range(2):
        own_bc(t).wait()
        arrived(t, 0).wait_recv()
    for k in range(1, NC):
        forward(k, False).wait_recv()

    def scan_state(first, keep, t, source, order):
        s_acc[...] = jnp.zeros_like(s_acc)

        def one(i, carry):
            c = order(i)
            r = rows_of(c, L)
            rows_t = jnp.transpose(bc_v[t, r, :])
            for p in range(W // 256):
                col = slice(256 * p, 256 * p + 256)
                now = s_acc[:, col]
                keep[c + first, :, col] = now.astype(BF)
                s_acc[:, col] = elw[c][:, col] * now + nn(rows_t, source[r, col])
            return carry

        lax.fori_loop(0, NC, one, 0)

    def to_joiner(src, dst, send_sem, recv_sem, k):
        return remote(src.at[slab_at(k)], dst.at[seq], send_sem.at[k], recv_sem.at[k], slab_dev(k))

    def from_slab(src, dst, send_sem, recv_sem, k):
        place = lax.rem(seq + NC - k, NC)
        return remote(src.at[place], dst.at[place], send_sem.at[k], recv_sem.at[k], slab_dev(k))

    scan_state(0, s_loc, 0, xw, lambda i: i)
    high = slab_decay.astype(BF).astype(F32)
    decay_rows = jnp.concatenate(
        [high, slab_decay - high, jnp.zeros((14, W), F32)], axis=0
    ).astype(BF)
    for d in range(NC):
        col = slice(128 * d, 128 * d + 128)
        sendf[d, 0:STATE] = s_acc[:, col].astype(BF)
        sendf[d, STATE : STATE + 16] = decay_rows[:, col]
    for k in range(1, NC):
        to_joiner(sendf, recvf, xf_send, xf_recv, k).start()
    recvf[seq] = sendf[seq]

    scan_state(1, ds_loc, 1, dyw, lambda i: NC - 1 - i)
    for p in range(W // 256):
        col = slice(256 * p, 256 * p + 256)
        ds_loc[0, :, col] = s_acc[:, col].astype(BF)
    for d in range(NC):
        sendg[d] = s_acc[:, 128 * d : 128 * d + 128].astype(BF)
    for k in range(1, NC):
        to_joiner(sendg, recvg, xg_send, xg_recv, k).start()
    recvg[seq] = sendg[seq]

    low = iota0 >= iota1
    lane = lax.broadcasted_iota(jnp.int32, (1, L), 1)
    left = (lane < HEAD_DIM).astype(F32)
    left_b = left.astype(BF)
    right_b = (1.0 - left).astype(BF)

    def intra(c, carry):
        r = rows_of(c, L)
        b_c, c_c = bc_v[0, r, :], bc_v[1, r, :]
        scores = jnp.where(low, nt(c_c, b_c), 0.0)
        d_scores = jnp.zeros((L, L), F32)
        cum_r, cum_c = cumv[c], cumt[c]
        for p in range(H // 2):
            col = slice(L * p, L * p + L)
            x_p, dy_p = xp[r, col], dy[r, col]
            x_two = jnp.concatenate([x_p * left_b, x_p * right_b], axis=0)
            d_mix = nt(dy_p, x_two)
            parts = []
            for j in range(2):
                h = 2 * p + j
                seg = cum_c[:, h : h + 1] - cum_r[h : h + 1, :]
                mask = jnp.exp2(jnp.minimum(seg, 0.0))
                parts.append((scores * mask).astype(BF))
                d_scores = d_scores + d_mix[:, L * j : L * j + L] * mask
            mix = jnp.concatenate(parts, axis=1)
            yd[r, col] = nn(mix, x_two)
            both = tn(mix, dy_p)
            dxd[r, col] = jnp.where(left > 0.0, both[:L], both[L:])
        d_scores = jnp.where(low, d_scores, 0.0).astype(BF)
        stage[c, 0] = tn(d_scores, c_c)
        stage[c, 1] = nn(d_scores, b_c)
        return carry

    lax.fori_loop(0, NC // 2, intra, 0)

    for k in range(1, NC):
        from_slab(sendf, recvf, xf_send, xf_recv, k).wait_recv()
    run = jnp.zeros((STATE, L), F32)
    for i in range(NC):
        outf[i] = run.astype(BF)
        factor = recvf[i, STATE : STATE + 16].astype(F32)
        run = (factor[0:1] + factor[1:2]) * run + recvf[i, 0:STATE].astype(F32)

    def back(src, dst, send_sem, recv_sem, k):
        return remote(
            src.at[slab_at(k)], dst.at[seq], send_sem.at[k], recv_sem.at[k], slab_dev(k)
        )

    for k in range(1, NC):
        back(outf, s_in, rf_send, rf_recv, k).start()
    s_in[seq] = outf[seq]
    for k in range(1, NC):
        from_slab(sendg, recvg, xg_send, xg_recv, k).wait_recv()
    run = jnp.zeros((STATE, L), F32)
    for i in reversed(range(NC)):
        outg[i] = run.astype(BF)
        factor = recvf[i, STATE : STATE + 16].astype(F32)
        run = (factor[0:1] + factor[1:2]) * run + recvg[i].astype(F32)
    for k in range(1, NC):
        back(outg, ds_in, rg_send, rg_recv, k).start()
    ds_in[seq] = outg[seq]

    lax.fori_loop(NC // 2, NC, intra, 0)

    for k in range(1, NC):
        from_slab(outf, s_in, rf_send, rf_recv, k).wait_recv()
        from_slab(outg, ds_in, rg_send, rg_recv, k).wait_recv()

    def to_sibling(k):
        c = chip_at(k)
        return remote(
            stage.at[c, :, rows_of(1 - core, ROWS)], sib.at[c], sib_send.at[k], sib_recv.at[k], sibling
        )

    def to_owner(k):
        return remote(
            fin.at[chip_at(k)],
            gbc.at[:, :, rows_of(chip, STATE)],
            fin_send.at[k],
            fin_recv.at[k],
            chip_dev(k),
        )

    def from_group(k):
        return remote(
            fin.at[chip_at(k)],
            gbc.at[:, :, rows_of(lax.rem(chip + NC - k, NC), STATE)],
            fin_send.at[k],
            fin_recv.at[k],
            sibling,
        )

    def store(a, c):
        src, dst = ((x_v, gx_hbm), (z_v, gated_hbm), (g_v, gz_hbm))[a]
        return pltpu.make_async_copy(
            src.at[rows_of(c, L)], dst.at[rows_of(c, L)], out_sem.at[a, c]
        )

    def settle(k):
        c = chip_at(k)
        to_sibling(k).wait_recv()
        total = (stage[c, :, rows_of(core, ROWS)] + sib[c]).astype(BF)

        @pl.when(k == 0)
        def _():
            gbc[:, :, rows_of(chip, STATE)] = total

        @pl.when(k > 0)
        def _():
            fin[c] = total
            to_owner(k).start()

    def finish(k, carry):
        c = chip_at(k)
        r = rows_of(c, L)
        b_c, c_c = bc_v[0, r, :], bc_v[1, r, :]
        d_b, d_c = stage[c, 0], stage[c, 1]
        q = jnp.zeros((H, L), F32)
        px = jnp.zeros((H, L), F32)
        for p in range(W // 256):
            col = slice(256 * p, 256 * p + 256)
            start = jnp.concatenate([s_in[2 * p], s_in[2 * p + 1]], axis=1).astype(F32)
            end = jnp.concatenate([ds_in[2 * p], ds_in[2 * p + 1]], axis=1).astype(F32)
            s_t = s_loc[c, :, col].astype(F32) + prew[c][:, col] * start
            ds_t = ds_loc[c + 1, :, col].astype(F32) + postw[c + 1][:, col] * end
            ds_p = ds_loc[c, :, col].astype(F32) + postw[c][:, col] * end
            fw[c, :, col] = jnp.sum(s_t * ds_p, axis=0, keepdims=True)
            s_b, ds_b = s_t.astype(BF), ds_t.astype(BF)
            d_c = d_c + nt(dyw[r, col], s_b)
            d_b = d_b + nt(xw[r, col], ds_b)
            y_core = yd[r, col] + ecw[r, col].astype(F32) * nn(c_c, s_b)
            dx = dxd[r, col] + ww[r, col].astype(F32) * nn(b_c, ds_b)
            e_c = e_s[:, col]
            p_x = xp[r, col].astype(F32) * dx
            q_x = dy[r, col].astype(F32) * y_core - p_x
            q_h = q_x.astype(BF)
            q_l = (q_x - q_h.astype(F32)).astype(BF)
            q = q + nt(e_c, q_h) + nt(e_c, q_l)
            px = px + nt(e_c, p_x.astype(BF))
            x, z, g = (v[r, col].astype(F32) for v in (x_v, z_v, g_v))
            skip = skw[:, col]
            sig = 1.0 / (1.0 + jnp.exp(-z))
            silu = z * sig
            y = y_core + skip * x
            dy_f = g * silu
            z_v[r, col] = (y * silu).astype(BF)
            g_v[r, col] = (g * y * (sig + silu * (1.0 - sig))).astype(BF)
            x_v[r, col] = (skip * dy_f + dtw[r, col].astype(F32) * dx).astype(BF)
            skipacc[:, col] += jnp.sum((dy_f * x).reshape(L // 8, 8, 256), axis=0)
        stage[c, 0] = d_b
        stage[c, 1] = d_c
        qs[c] = q
        ps[c] = px
        for a in range(3):
            store(a, c).start()
        to_sibling(k).start()

        @pl.when(k > 0)
        def _():
            settle(k - 1)

        return carry

    lax.fori_loop(0, NC, finish, 0)
    settle(NC - 1)

    q = qs[...].reshape(L, L)
    px = ps[...].reshape(L, L)
    before = dot(q, (iota0 < iota1).astype(F32), 1, 0, HIGHEST)
    pairs = dot(spread_f, fw[...].reshape(NC, W), 1, 1, HIGHEST)
    boundary = jnp.concatenate([pairs[:, c : c + 1] for c in range(NC)], axis=0)
    d_decay = boundary - before
    d_step = px / step_r.astype(F32) + rate * d_decay
    d_raw = d_step / (1.0 + jnp.exp(-pre))
    for c in range(NC):
        gdt_ref[:, L * c : L * c + L] = d_raw[H * c : H * c + H].astype(BF)

    def over_tokens(v):
        column = jnp.sum(v, axis=1, keepdims=True)
        total = column[0:H]
        for c in range(1, NC):
            total = total + column[H * c : H * c + H]
        return total

    skip_sum = jnp.sum(dot(spread_f, skipacc[...], 1, 1, HIGHEST), axis=1, keepdims=True)
    lane16 = lax.broadcasted_iota(jnp.int32, (H, L), 1)
    par[0] = jnp.where(
        lane16 == 0,
        over_tokens(d_decay * decay),
        jnp.where(lane16 == 1, over_tokens(d_raw), skip_sum),
    )

    def share(k):
        return remote(par.at[0], par.at[k], par_send.at[k], par_recv.at[k], slab_dev(k))

    for k in range(1, NC):
        share(k).start()
    for k in range(1, NC):
        from_group(k).wait_recv()
    outs = [
        pltpu.make_async_copy(gbc.at[0], gb_hbm, gout_sem.at[0]),
        pltpu.make_async_copy(gbc.at[1], gc_hbm, gout_sem.at[1]),
    ]
    for o in outs:
        o.start()
    for k in range(1, NC):
        share(k).wait_recv()
    total = par[0]
    for k in range(1, NC):
        total = total + par[k]
    flat = jnp.transpose(jnp.concatenate([total] * NC, axis=0))
    galog_ref[...] = flat[0:1, 0:H]
    gbias_ref[...] = flat[1:2, 0:H]
    gskip_ref[...] = flat[2:3, 0:H]

    for o in outs:
        o.wait()
    for k in range(NC):
        for t in range(2):
            spread(t, k).wait_send()
        to_sibling(k).wait_send()
    for k in range(1, NC):
        forward(k, True).wait_send()
        to_joiner(sendf, recvf, xf_send, xf_recv, k).wait_send()
        to_joiner(sendg, recvg, xg_send, xg_recv, k).wait_send()
        back(outf, s_in, rf_send, rf_recv, k).wait_send()
        back(outg, ds_in, rg_send, rg_recv, k).wait_send()
        to_owner(k).wait_send()
        share(k).wait_send()
    for c in range(NC):
        for a in range(3):
            store(a, c).wait()


def per_device(inner_x, gate_z, dt_raw, b_proj, c_proj, a_log, dt_bias, d_skip, grad_gated):
    tokens = inner_x.shape[0]
    any_space = pl.BlockSpec(memory_space=pl.ANY)
    vmem = pl.BlockSpec(memory_space=pltpu.VMEM)
    smem = pl.BlockSpec(memory_space=pltpu.SMEM)
    sem = pltpu.SemaphoreType.DMA
    big = jax.ShapeDtypeStruct((tokens, W), BF)
    rows = jax.ShapeDtypeStruct((ROWS, GROUPS * STATE), BF)
    head = jax.ShapeDtypeStruct((1, H), F32)
    wide = pltpu.VMEM((tokens, W), BF)
    scratch = [
        wide, wide, wide,
        wide, wide, wide, wide,
        wide, wide, wide,
        pltpu.VMEM((H, W), BF),
        pltpu.VMEM((NC, L, H), BF),
        pltpu.VMEM((NC, L, H), BF),
        pltpu.VMEM((NC, L, H), BF),
        pltpu.VMEM((NC, H, L), F32),
        pltpu.VMEM((NC, L, H), F32),
        pltpu.VMEM((NC, 1, W), F32),
        pltpu.VMEM((NC, 1, W), F32),
        pltpu.VMEM((NC + 1, 1, W), F32),
        pltpu.VMEM((1, W), F32),
        pltpu.VMEM((2, tokens, STATE), BF),
        pltpu.VMEM((NC, STATE, W), BF),
        pltpu.VMEM((NC + 1, STATE, W), BF),
        pltpu.VMEM((STATE, W), F32),
        pltpu.VMEM((tokens, W), F32),
        pltpu.VMEM((tokens, W), F32),
        pltpu.VMEM((NC, 2, L, STATE), F32),
        pltpu.VMEM((NC, 2, ROWS, STATE), F32),
        pltpu.VMEM((NC, 2, ROWS, STATE), BF),
        pltpu.VMEM((2, ROWS, GROUPS * STATE), BF),
        pltpu.VMEM((NC, STATE + 16, L), BF),
        pltpu.VMEM((NC, STATE, L), BF),
        pltpu.VMEM((NC, STATE + 16, L), BF),
        pltpu.VMEM((NC, STATE, L), BF),
        pltpu.VMEM((NC, STATE, L), BF),
        pltpu.VMEM((NC, STATE, L), BF),
        pltpu.VMEM((NC, STATE, L), BF),
        pltpu.VMEM((NC, STATE, L), BF),
        pltpu.VMEM((8, W), F32),
        pltpu.VMEM((NC, 1, W), F32),
        pltpu.VMEM((NC, H, L), F32),
        pltpu.VMEM((NC, H, L), F32),
        pltpu.VMEM((NC, H, L), F32),
        sem((3, NC)), sem((3, NC)), sem((2,)),
        sem((2, NC)), sem((2, NC)), sem((NC,)), sem((NC,)),
        sem((NC,)), sem((NC,)), sem((NC,)), sem((NC,)),
        sem((NC,)), sem((NC,)), sem((NC,)), sem((NC,)),
        sem((NC,)), sem((NC,)), sem((NC,)), sem((NC,)), sem((NC,)), sem((NC,)),
        sem((2,)),
    ]
    outs = pl.pallas_call(
        kernel,
        out_shape=(big, big, big, jax.ShapeDtypeStruct((H, tokens), BF), rows, rows, head, head, head),
        in_specs=[any_space, any_space, any_space, vmem, any_space, any_space, smem, smem, smem],
        out_specs=(any_space, any_space, any_space, vmem, any_space, any_space, vmem, vmem, vmem),
        scratch_shapes=scratch,
        compiler_params=pltpu.CompilerParams(
            collective_id=0, has_side_effects=True, vmem_limit_bytes=60 * 2**20
        ),
    )(inner_x, gate_z, grad_gated, dt_raw, b_proj, c_proj, a_log, dt_bias, d_skip)
    gated, grad_x, grad_z, grad_dt, grad_b, grad_c, g_alog, g_bias, g_skip = outs
    return (
        gated, grad_x, grad_z, grad_dt, grad_b, grad_c,
        g_alog.reshape(H), g_bias.reshape(H), g_skip.reshape(H),
    )


def solution(mesh):
    in_specs = (
        P("seq", "head"),
        P("seq", "head"),
        P("head", "seq"),
        P(("seq", "head"), None),
        P(("seq", "head"), None),
        P("head"),
        P("head"),
        P("head"),
        P("seq", "head"),
    )
    out_specs = (
        P("seq", "head"),
        P("seq", "head"),
        P("seq", "head"),
        P("head", "seq"),
        P(("seq", "head"), None),
        P(("seq", "head"), None),
        P("head"),
        P("head"),
        P("head"),
    )
    return jax.shard_map(
        per_device, mesh=mesh, in_specs=in_specs, out_specs=out_specs, check_vma=False
    )
```

```python
import jax
import jax.numpy as jnp
from jax import lax
from jax.experimental import pallas as pl
from jax.experimental.pallas import tpu as pltpu
from jax.sharding import PartitionSpec as P

HEAD_DIM = 64
STATE = 256
GROUPS = 8
L = 128
NC = 8
H = 16
W = H * HEAD_DIM
ROWS = 64
F32, BF = jnp.float32, jnp.bfloat16
MESH = pl.DeviceIdType.MESH
HIGHEST = lax.Precision.HIGHEST
AROUND = (5, 4, 3, 2, 7, 6, 1)
LOG2E = 1.4426950408889634


def dot(a, b, ca, cb, precision=None):
    return lax.dot_general(
        a, b, (((ca,), (cb,)), ((), ())), preferred_element_type=F32, precision=precision
    )


def nn(a, b):
    return dot(a, b, 1, 0)


def nt(a, b):
    return dot(a, b, 1, 1)


def tn(a, b):
    return dot(a, b, 0, 0)


def remote(src, dst, send_sem, recv_sem, device):
    return pltpu.make_async_remote_copy(
        src_ref=src,
        dst_ref=dst,
        send_sem=send_sem,
        recv_sem=recv_sem,
        device_id=device,
        device_id_type=MESH,
    )


def rows_of(index, count):
    return pl.ds(pl.multiple_of(index * count, count), count)


def kernel(
    x_hbm, z_hbm, g_hbm, dt_ref, b_hbm, c_hbm, alog_ref, bias_ref, skip_ref,
    gated_hbm, gx_hbm, gz_hbm, gdt_ref, gb_hbm, gc_hbm, galog_ref, gbias_ref, gskip_ref,
    x_v, z_v, g_v, xp, dy, xw, dyw, dtw, ecw, ww, e_s, dtv, ecv, wv, cumv, cumt,
    elw, prew, postw, skw, bc_v, s_loc, ds_loc, s_acc, yd, dxd, stage, sib, fin, gbc,
    sendf, sendg, recvf, recvg, outf, outg, s_in, ds_in, skipacc, fw, qs, ps, par,
    in_sem, out_sem, loc_sem, a_send, a_recv, f_send, f_recv, xf_send, xf_recv, xg_send, xg_recv,
    rf_send, rf_recv, rg_send, rg_recv, sib_send, sib_recv, fin_send, fin_recv, par_send, par_recv,
    gout_sem,
):
    seq = lax.axis_index("seq")
    hd = lax.axis_index("head")
    core = hd & 1
    chip = hd >> 1
    sibling = (seq, 2 * chip + 1 - core)

    def chip_at(k):
        return ((chip + k) & 3) | ((chip ^ k) & 4)

    def chip_back(k):
        return ((chip - k) & 3) | ((chip ^ k) & 4)

    def chip_dev(k):
        return (seq, 2 * chip_at(k) + core)

    def slab_at(k):
        return ((seq + (k & 6)) & 6) | ((seq ^ k) & 1)

    def slab_back(k):
        return ((seq - (k & 6)) & 6) | ((seq ^ k) & 1)

    def slab_dev(k):
        return (slab_at(k), hd)

    def load(a, c):
        src, dst = ((x_hbm, x_v), (z_hbm, z_v), (g_hbm, g_v))[a]
        return pltpu.make_async_copy(
            src.at[rows_of(c, L)], dst.at[rows_of(c, L)], in_sem.at[a, c]
        )

    def own_bc(t):
        src = (b_hbm, c_hbm)[t]
        return pltpu.make_async_copy(
            src.at[:, rows_of(chip, STATE)], bc_v.at[t, rows_of(hd, ROWS)], loc_sem.at[t]
        )

    for c in range(NC):
        for a in range(3):
            load(a, c).start()
    for t in range(2):
        own_bc(t).start()

    barrier = pltpu.get_barrier_semaphore()
    for k in range(1, NC):
        pl.semaphore_signal(barrier, inc=1, device_id=chip_dev(k), device_id_type=MESH)
        pl.semaphore_signal(barrier, inc=1, device_id=slab_dev(k), device_id_type=MESH)
    pl.semaphore_signal(barrier, inc=1, device_id=sibling, device_id_type=MESH)
    pl.semaphore_wait(barrier, 2 * NC - 1)

    def spread(t, k):
        src = (b_hbm, c_hbm)[t]
        device = sibling if k == 0 else chip_dev(k)
        group = chip if k == 0 else chip_at(k)
        return remote(
            src.at[:, rows_of(group, STATE)],
            bc_v.at[t, rows_of(hd, ROWS)],
            a_send.at[t, k],
            a_recv.at[t, k],
            device,
        )

    def arrived(t, k):
        place = 2 * chip + 1 - core if k == 0 else 2 * chip_back(k) + core
        return remote(
            b_hbm.at[:, rows_of(chip, STATE)],
            bc_v.at[t, rows_of(place, ROWS)],
            a_send.at[t, k],
            a_recv.at[t, k],
            sibling,
        )

    def forward(t, k, mine):
        place = 2 * chip_back(k) + (core if mine else 1 - core)
        block = bc_v.at[t, rows_of(place, ROWS)]
        return remote(block, block, f_send.at[t, k], f_recv.at[t, k], sibling)

    for t in range(2):
        for k in (6, 5, 7, 4, 2, 1, 3, 0):
            spread(t, k).start()

    def pass_on(t):
        for k in (4, 1, 3, 2, 5, 7, 6):
            arrived(t, k).wait_recv()
            forward(t, k, True).start()

    def complete(t):
        own_bc(t).wait()
        arrived(t, 0).wait_recv()
        for k in range(1, NC):
            forward(t, k, False).wait_recv()

    row16 = lax.broadcasted_iota(jnp.int32, (H, L), 0)

    def per_head(ref):
        column = jnp.zeros((H, L), F32)
        for h in range(H):
            column = jnp.where(row16 == h, ref[h], column)
        return jnp.concatenate([column] * NC, axis=0)

    rate = -jnp.exp(per_head(alog_ref))
    raw = dt_ref[...].astype(F32)
    pre = jnp.concatenate([raw[:, L * c : L * c + L] for c in range(NC)], axis=0) + per_head(bias_ref)
    step = jnp.maximum(pre, 0.0) + jnp.log1p(jnp.exp(-jnp.abs(pre)))
    decay = rate * step
    iota0 = lax.broadcasted_iota(jnp.int32, (L, L), 0)
    iota1 = lax.broadcasted_iota(jnp.int32, (L, L), 1)
    upper = (iota0 <= iota1).astype(F32)
    cum = dot(decay, upper, 1, 0, HIGHEST)
    ecum = jnp.exp(cum)
    tail = jnp.exp(cum[:, L - 1 : L] - cum)
    cum2 = cum * LOG2E
    cum_t = jnp.transpose(cum2)
    step_t = jnp.transpose(step)
    ecum_t = jnp.transpose(ecum)
    tail_t = jnp.transpose(tail)
    for c in range(NC):
        cumv[c] = cum2[H * c : H * c + H]
        cumt[c] = cum_t[:, H * c : H * c + H]
        for keep, value in ((dtv, step_t), (ecv, ecum_t), (wv, tail_t)):
            column = value[:, H * c : H * c + H]
            high = column.astype(BF)
            keep[c] = jnp.concatenate([high.astype(F32), column - high.astype(F32)], axis=1).astype(BF)
    head_of = lax.shift_right_logical(lax.broadcasted_iota(jnp.int32, (H, W), 1), 6)
    onehot = head_of == lax.broadcasted_iota(jnp.int32, (H, W), 0)
    spread_f = onehot.astype(F32)
    e_s[...] = jnp.concatenate([spread_f, spread_f], axis=0).astype(BF)
    last8 = jnp.concatenate([ecum_t[L - 1 : L, H * c : H * c + H] for c in range(NC)], axis=0)
    elast = dot(last8, spread_f, 1, 0, HIGHEST)
    skip_row = jnp.zeros((1, W), F32)
    for h in range(H):
        skip_row = jnp.where(head_of[0:1] == h, skip_ref[h], skip_row)
    skw[...] = skip_row
    run = jnp.ones((1, W), F32)
    for c in range(NC):
        elw[c] = elast[c : c + 1]
        prew[c] = run
        run = run * elast[c : c + 1]
    slab_decay = run
    run = jnp.ones((1, W), F32)
    for c in reversed(range(NC)):
        postw[c + 1] = run
        run = run * elast[c : c + 1]
    postw[0] = run
    skipacc[...] = jnp.zeros_like(skipacc)

    def prepare_x(c, carry):
        load(0, c).wait()
        r = rows_of(c, L)
        dt_c, w_c = dtv[c], wv[c]
        for p in range(W // 256):
            col = slice(256 * p, 256 * p + 256)
            e_c = e_s[:, col]
            dt_w, w_w = nn(dt_c, e_c), nn(w_c, e_c)
            dtw[r, col] = dt_w
            ww[r, col] = w_w
            scaled = x_v[r, col].astype(F32) * dt_w
            xp[r, col] = scaled.astype(BF)
            xw[r, col] = (scaled * w_w).astype(BF)
        return carry

    def prepare_g(c, carry):
        load(1, c).wait()
        load(2, c).wait()
        r = rows_of(c, L)
        ec_c = ecv[c]
        for p in range(W // 256):
            col = slice(256 * p, 256 * p + 256)
            ec_w = nn(ec_c, e_s[:, col])
            ecw[r, col] = ec_w
            z = z_v[r, col].astype(F32)
            dy_f = g_v[r, col].astype(F32) * (z / (1.0 + jnp.exp(-z)))
            dy[r, col] = dy_f.astype(BF)
            dyw[r, col] = (dy_f * ec_w).astype(BF)
        return carry

    lax.fori_loop(0, NC, prepare_x, 0)
    pass_on(0)
    complete(0)

    def scan_state(first, keep, t, source, order):
        s_acc[...] = jnp.zeros_like(s_acc)

        def one(i, carry):
            c = order(i)
            r = rows_of(c, L)
            rows_t = jnp.transpose(bc_v[t, r, :])
            for p in range(W // 256):
                col = slice(256 * p, 256 * p + 256)
                now = s_acc[:, col]
                keep[c + first, :, col] = now.astype(BF)
                s_acc[:, col] = elw[c][:, col] * now + nn(rows_t, source[r, col])
            return carry

        lax.fori_loop(0, NC, one, 0)

    def to_joiner(src, dst, send_sem, recv_sem, k):
        return remote(src.at[slab_at(k)], dst.at[seq], send_sem.at[k], recv_sem.at[k], slab_dev(k))

    def from_slab(src, dst, send_sem, recv_sem, k):
        place = slab_back(k)
        return remote(src.at[place], dst.at[place], send_sem.at[k], recv_sem.at[k], slab_dev(k))

    scan_state(0, s_loc, 0, xw, lambda i: i)
    high = slab_decay.astype(BF).astype(F32)
    decay_rows = jnp.concatenate(
        [high, slab_decay - high, jnp.zeros((14, W), F32)], axis=0
    ).astype(BF)
    for d in range(NC):
        col = slice(128 * d, 128 * d + 128)
        sendf[d, 0:STATE] = s_acc[:, col].astype(BF)
        sendf[d, STATE : STATE + 16] = decay_rows[:, col]
    @pl.when(seq != NC - 1)
    def _():
        for k in AROUND:
            to_joiner(sendf, recvf, xf_send, xf_recv, k).start()

    recvf[seq] = sendf[seq]

    pass_on(1)
    lax.fori_loop(0, NC, prepare_g, 0)
    complete(1)
    scan_state(1, ds_loc, 1, dyw, lambda i: NC - 1 - i)
    for p in range(W // 256):
        col = slice(256 * p, 256 * p + 256)
        ds_loc[0, :, col] = s_acc[:, col].astype(BF)
    for d in range(NC):
        sendg[d] = s_acc[:, 128 * d : 128 * d + 128].astype(BF)
    @pl.when(seq != 0)
    def _():
        for k in AROUND:
            to_joiner(sendg, recvg, xg_send, xg_recv, k).start()

    recvg[seq] = sendg[seq]

    low = iota0 >= iota1
    lane = lax.broadcasted_iota(jnp.int32, (1, L), 1)
    left = (lane < HEAD_DIM).astype(F32)
    left_b = left.astype(BF)
    right_b = (1.0 - left).astype(BF)

    def by_head(v, col):
        high = v.astype(BF)
        low_part = (v - high.astype(F32)).astype(BF)
        e_c = e_s[0:H, col]
        return nt(e_c, high) + nt(e_c, low_part)

    def intra(c, carry):
        r = rows_of(c, L)
        b_c, c_c = bc_v[0, r, :], bc_v[1, r, :]
        scores = jnp.where(low, nt(c_c, b_c), 0.0)
        d_scores = jnp.zeros((L, L), F32)
        px = jnp.zeros((H, L), F32)
        cum_r, cum_c = cumv[c], cumt[c]
        for p in range(H // 2):
            col = slice(L * p, L * p + L)
            x_p, dy_p = xp[r, col], dy[r, col]
            x_two = jnp.concatenate([x_p * left_b, x_p * right_b], axis=0)
            d_mix = nt(dy_p, x_two)
            parts = []
            for j in range(2):
                h = 2 * p + j
                seg = cum_c[:, h : h + 1] - cum_r[h : h + 1, :]
                mask = jnp.exp2(jnp.minimum(seg, 0.0))
                parts.append((scores * mask).astype(BF))
                d_scores = d_scores + d_mix[:, L * j : L * j + L] * mask
            mix = jnp.concatenate(parts, axis=1)
            yd[r, col] = nn(mix, x_two)
            both = tn(mix, dy_p)
            dx = jnp.where(left > 0.0, both[:L], both[L:])
            dxd[r, col] = dx
            px = px + by_head(x_p.astype(F32) * dx, col)
        d_scores = jnp.where(low, d_scores, 0.0).astype(BF)
        stage[c, 0] = tn(d_scores, c_c)
        stage[c, 1] = nn(d_scores, b_c)
        ps[c] = px
        return carry

    lax.fori_loop(0, 3, intra, 0)

    def collect(src, dst, send_sem, recv_sem, absent):
        for k in range(1, NC):

            @pl.when(slab_back(k) != absent)
            def _():
                from_slab(src, dst, send_sem, recv_sem, k).wait_recv()

    collect(sendf, recvf, xf_send, xf_recv, NC - 1)
    run = jnp.zeros((STATE, L), F32)
    for i in range(NC):
        outf[i] = run.astype(BF)
        if i == 0:
            run = recvf[0, 0:STATE].astype(F32)
        elif i < NC - 1:
            factor = recvf[i, STATE : STATE + 16].astype(F32)
            run = (factor[0:1] + factor[1:2]) * run + recvf[i, 0:STATE].astype(F32)

    def back(src, dst, send_sem, recv_sem, k):
        return remote(
            src.at[slab_at(k)], dst.at[seq], send_sem.at[k], recv_sem.at[k], slab_dev(k)
        )

    def give_back(src, dst, send_sem, recv_sem, absent):
        for k in AROUND:

            @pl.when(slab_at(k) != absent)
            def _():
                back(src, dst, send_sem, recv_sem, k).start()

    give_back(outf, s_in, rf_send, rf_recv, 0)
    s_in[seq] = outf[seq]
    lax.fori_loop(3, 6, intra, 0)
    collect(sendg, recvg, xg_send, xg_recv, 0)
    run = jnp.zeros((STATE, L), F32)
    for i in reversed(range(NC)):
        outg[i] = run.astype(BF)
        if i == NC - 1:
            run = recvg[i].astype(F32)
        elif i > 0:
            factor = recvf[i, STATE : STATE + 16].astype(F32)
            run = (factor[0:1] + factor[1:2]) * run + recvg[i].astype(F32)
    give_back(outg, ds_in, rg_send, rg_recv, NC - 1)
    ds_in[seq] = outg[seq]

    lax.fori_loop(6, NC, intra, 0)

    def to_sibling(t, k):
        c = chip_at(k)
        return remote(
            stage.at[c, t, rows_of(1 - core, ROWS)],
            sib.at[c, t],
            sib_send.at[t, k],
            sib_recv.at[t, k],
            sibling,
        )

    def to_owner(t, k):
        return remote(
            fin.at[chip_at(k), t],
            gbc.at[t, :, rows_of(chip, STATE)],
            fin_send.at[t, k],
            fin_recv.at[t, k],
            chip_dev(k),
        )

    def from_group(t, k):
        return remote(
            fin.at[chip_at(k), t],
            gbc.at[t, :, rows_of(chip_back(k), STATE)],
            fin_send.at[t, k],
            fin_recv.at[t, k],
            sibling,
        )

    def store(a, c):
        src, dst = ((x_v, gx_hbm), (z_v, gated_hbm), (g_v, gz_hbm))[a]
        return pltpu.make_async_copy(
            src.at[rows_of(c, L)], dst.at[rows_of(c, L)], out_sem.at[a, c]
        )

    def settle(t, k):
        c = chip_at(k)
        to_sibling(t, k).wait_recv()
        total = (stage[c, t, rows_of(core, ROWS)] + sib[c, t]).astype(BF)

        @pl.when(k == 0)
        def _():
            gbc[t, :, rows_of(chip, STATE)] = total

        @pl.when(k > 0)
        def _():
            fin[c, t] = total
            to_owner(t, k).start()

    def finish_y(k, carry):
        c = chip_at(k)
        r = rows_of(c, L)
        c_c = bc_v[1, r, :]
        d_c = stage[c, 1]
        q = jnp.zeros((H, L), F32)
        for p in range(W // 256):
            col = slice(256 * p, 256 * p + 256)
            start = jnp.concatenate([s_in[2 * p], s_in[2 * p + 1]], axis=1).astype(F32)
            s_b = (s_loc[c, :, col].astype(F32) + prew[c][:, col] * start).astype(BF)
            s_loc[c, :, col] = s_b
            d_c = d_c + nt(dyw[r, col], s_b)
            y_core = yd[r, col] + ecw[r, col] * nn(c_c, s_b)
            q = q + by_head(dy[r, col].astype(F32) * y_core, col)
            x, z, g = (v[r, col].astype(F32) for v in (x_v, z_v, g_v))
            sig = 1.0 / (1.0 + jnp.exp(-z))
            silu = z * sig
            y = y_core + skw[:, col] * x
            z_v[r, col] = (y * silu).astype(BF)
            g_v[r, col] = (g * y * (sig + silu * (1.0 - sig))).astype(BF)
            skipacc[:, col] += jnp.sum((g * silu * x).reshape(L // 8, 8, 256), axis=0)
        stage[c, 1] = d_c
        qs[c] = q
        store(1, c).start()
        store(2, c).start()
        to_sibling(1, k).start()
        return carry

    def finish_b(k, carry):
        c = chip_at(k)
        r = rows_of(c, L)
        d_b = stage[c, 0]
        for p in range(W // 256):
            col = slice(256 * p, 256 * p + 256)
            end = jnp.concatenate([ds_in[2 * p], ds_in[2 * p + 1]], axis=1).astype(F32)
            ds_b = (ds_loc[c + 1, :, col].astype(F32) + postw[c + 1][:, col] * end).astype(BF)
            ds_loc[c + 1, :, col] = ds_b
            d_b = d_b + nt(xw[r, col], ds_b)
        stage[c, 0] = d_b
        to_sibling(0, k).start()
        return carry

    def finish_x(c, carry):
        r = rows_of(c, L)
        b_c = bc_v[0, r, :]
        px = jnp.zeros((H, L), F32)
        for p in range(W // 256):
            col = slice(256 * p, 256 * p + 256)
            pair = s_loc[c, :, col].astype(F32) * ds_loc[c, :, col].astype(F32)
            fw[c, :, col] = jnp.sum(pair, axis=0, keepdims=True)
            off = ww[r, col] * nn(b_c, ds_loc[c + 1, :, col])
            px = px + nt(e_s[0:H, col], (xp[r, col].astype(F32) * off).astype(BF))
            dx = dxd[r, col] + off
            x_v[r, col] = (skw[:, col] * dy[r, col].astype(F32) + dtw[r, col] * dx).astype(BF)
        total = ps[c] + px
        ps[c] = total
        qs[c] = qs[c] - total
        store(0, c).start()
        return carry

    def settle_all(t):
        def one(k, carry):
            settle(t, k)
            return carry

        lax.fori_loop(0, NC, one, 0)

    @pl.when(seq == 0)
    def _():
        s_in[...] = jnp.zeros_like(s_in)

    @pl.when(seq != 0)
    def _():
        for k in range(1, NC):
            from_slab(outf, s_in, rf_send, rf_recv, k).wait_recv()

    lax.fori_loop(0, NC, finish_y, 0)
    settle_all(1)

    @pl.when(seq == NC - 1)
    def _():
        ds_in[...] = jnp.zeros_like(ds_in)

    @pl.when(seq != NC - 1)
    def _():
        for k in range(1, NC):
            from_slab(outg, ds_in, rg_send, rg_recv, k).wait_recv()

    lax.fori_loop(0, NC, finish_b, 0)
    settle_all(0)
    for p in range(W // 256):
        col = slice(256 * p, 256 * p + 256)
        end = jnp.concatenate([ds_in[2 * p], ds_in[2 * p + 1]], axis=1).astype(F32)
        ds_loc[0, :, col] = (ds_loc[0, :, col].astype(F32) + postw[0][:, col] * end).astype(BF)
    lax.fori_loop(0, NC, finish_x, 0)

    q = qs[...].reshape(L, L)
    px = ps[...].reshape(L, L)
    before = dot(q, (iota0 < iota1).astype(F32), 1, 0, HIGHEST)
    pairs = dot(spread_f, fw[...].reshape(NC, W), 1, 1, HIGHEST)
    boundary = jnp.concatenate([pairs[:, c : c + 1] for c in range(NC)], axis=0)
    d_decay = boundary - before
    d_step = px / step + rate * d_decay
    d_raw = d_step / (1.0 + jnp.exp(-pre))
    for c in range(NC):
        gdt_ref[:, L * c : L * c + L] = d_raw[H * c : H * c + H].astype(BF)

    def over_tokens(v):
        column = jnp.sum(v, axis=1, keepdims=True)
        total = column[0:H]
        for c in range(1, NC):
            total = total + column[H * c : H * c + H]
        return total

    skip_sum = jnp.sum(dot(spread_f, skipacc[...], 1, 1, HIGHEST), axis=1, keepdims=True)
    lane16 = lax.broadcasted_iota(jnp.int32, (H, L), 1)
    par[0] = jnp.where(
        lane16 == 0,
        over_tokens(d_decay * decay),
        jnp.where(lane16 == 1, over_tokens(d_raw), skip_sum),
    )

    def share(k):
        return remote(par.at[0], par.at[k], par_send.at[k], par_recv.at[k], slab_dev(k))

    for k in range(1, NC):
        share(k).start()
    for k in range(1, NC):
        for t in range(2):
            from_group(t, k).wait_recv()
    outs = [
        pltpu.make_async_copy(gbc.at[0], gb_hbm, gout_sem.at[0]),
        pltpu.make_async_copy(gbc.at[1], gc_hbm, gout_sem.at[1]),
    ]
    for o in outs:
        o.start()
    for k in range(1, NC):
        share(k).wait_recv()
    total = par[0]
    for k in range(1, NC):
        total = total + par[k]
    flat = jnp.transpose(jnp.concatenate([total] * NC, axis=0))
    galog_ref[...] = flat[0:1, 0:H]
    gbias_ref[...] = flat[1:2, 0:H]
    gskip_ref[...] = flat[2:3, 0:H]

    for o in outs:
        o.wait()
    for k in range(NC):
        for t in range(2):
            spread(t, k).wait_send()
            to_sibling(t, k).wait_send()
    for k in range(1, NC):
        for t in range(2):
            forward(t, k, True).wait_send()
            to_owner(t, k).wait_send()

        @pl.when(seq != NC - 1)
        def _():
            to_joiner(sendf, recvf, xf_send, xf_recv, k).wait_send()

        @pl.when(seq != 0)
        def _():
            to_joiner(sendg, recvg, xg_send, xg_recv, k).wait_send()

        @pl.when(slab_at(k) != 0)
        def _():
            back(outf, s_in, rf_send, rf_recv, k).wait_send()

        @pl.when(slab_at(k) != NC - 1)
        def _():
            back(outg, ds_in, rg_send, rg_recv, k).wait_send()

        share(k).wait_send()
    for c in range(NC):
        for a in range(3):
            store(a, c).wait()


def hand_out(*refs):
    ins, outs, held, (in_sem, out_sem) = refs[:9], refs[9:18], refs[18:27], refs[27:]
    blocks = [(a, pl.ds(L * c, L), NC * a + c) for c in range(NC) for a in range(3)]
    blocks += [(a, slice(None), 3 * NC + a - 3) for a in range(3, 9)]
    loads = [pltpu.make_async_copy(ins[a].at[r], held[a].at[r], in_sem.at[s]) for a, r, s in blocks]
    stores = [pltpu.make_async_copy(held[a].at[r], outs[a].at[r], out_sem.at[s]) for a, r, s in blocks]
    for load in loads:
        load.start()
    for load, store in zip(loads, stores):
        load.wait()
        store.start()
    for store in stores:
        store.wait()


def per_device(inner_x, gate_z, dt_raw, b_proj, c_proj, a_log, dt_bias, d_skip, grad_gated):
    tokens = inner_x.shape[0]
    any_space = pl.BlockSpec(memory_space=pl.ANY)
    vmem = pl.BlockSpec(memory_space=pltpu.VMEM)
    smem = pl.BlockSpec(memory_space=pltpu.SMEM)
    sem = pltpu.SemaphoreType.DMA
    big = jax.ShapeDtypeStruct((tokens, W), BF)
    rows = jax.ShapeDtypeStruct((ROWS, GROUPS * STATE), BF)
    head = jax.ShapeDtypeStruct((1, H), F32)
    wide = pltpu.VMEM((tokens, W), BF)
    wide_f = pltpu.VMEM((tokens, W), F32)
    scratch = [
        wide, wide, wide,
        wide, wide, wide, wide,
        wide_f, wide_f, wide_f,
        pltpu.VMEM((2 * H, W), BF),
        pltpu.VMEM((NC, L, 2 * H), BF),
        pltpu.VMEM((NC, L, 2 * H), BF),
        pltpu.VMEM((NC, L, 2 * H), BF),
        pltpu.VMEM((NC, H, L), F32),
        pltpu.VMEM((NC, L, H), F32),
        pltpu.VMEM((NC, 1, W), F32),
        pltpu.VMEM((NC, 1, W), F32),
        pltpu.VMEM((NC + 1, 1, W), F32),
        pltpu.VMEM((1, W), F32),
        pltpu.VMEM((2, tokens, STATE), BF),
        pltpu.VMEM((NC, STATE, W), BF),
        pltpu.VMEM((NC + 1, STATE, W), BF),
        pltpu.VMEM((STATE, W), F32),
        pltpu.VMEM((tokens, W), F32),
        pltpu.VMEM((tokens, W), F32),
        pltpu.VMEM((NC, 2, L, STATE), F32),
        pltpu.VMEM((NC, 2, ROWS, STATE), F32),
        pltpu.VMEM((NC, 2, ROWS, STATE), BF),
        pltpu.VMEM((2, ROWS, GROUPS * STATE), BF),
        pltpu.VMEM((NC, STATE + 16, L), BF),
        pltpu.VMEM((NC, STATE, L), BF),
        pltpu.VMEM((NC, STATE + 16, L), BF),
        pltpu.VMEM((NC, STATE, L), BF),
        pltpu.VMEM((NC, STATE, L), BF),
        pltpu.VMEM((NC, STATE, L), BF),
        pltpu.VMEM((NC, STATE, L), BF),
        pltpu.VMEM((NC, STATE, L), BF),
        pltpu.VMEM((8, W), F32),
        pltpu.VMEM((NC, 1, W), F32),
        pltpu.VMEM((NC, H, L), F32),
        pltpu.VMEM((NC, H, L), F32),
        pltpu.VMEM((NC, H, L), F32),
        sem((3, NC)), sem((3, NC)), sem((2,)),
        sem((2, NC)), sem((2, NC)), sem((2, NC)), sem((2, NC)),
        sem((NC,)), sem((NC,)), sem((NC,)), sem((NC,)),
        sem((NC,)), sem((NC,)), sem((NC,)), sem((NC,)),
        sem((2, NC)), sem((2, NC)), sem((2, NC)), sem((2, NC)), sem((NC,)), sem((NC,)),
        sem((2,)),
    ]
    small = (jax.ShapeDtypeStruct((H, tokens), BF), rows, rows, head, head, head)
    outs = pl.pallas_call(
        kernel,
        out_shape=(big, big, big) + small,
        in_specs=[any_space, any_space, any_space, vmem, any_space, any_space, smem, smem, smem],
        out_specs=(any_space, any_space, any_space, vmem, any_space, any_space, vmem, vmem, vmem),
        scratch_shapes=scratch,
        compiler_params=pltpu.CompilerParams(
            collective_id=0, has_side_effects=True, vmem_limit_bytes=60 * 2**20
        ),
    )(inner_x, gate_z, grad_gated, dt_raw, b_proj, c_proj, a_log, dt_bias, d_skip)
    outs = pl.pallas_call(
        hand_out,
        out_shape=(big, big, big) + small,
        in_specs=[any_space] * 9,
        out_specs=(any_space,) * 9,
        scratch_shapes=[pltpu.VMEM(v.shape, v.dtype) for v in outs]
        + [sem((3 * NC + 6,)), sem((3 * NC + 6,))],
        compiler_params=pltpu.CompilerParams(vmem_limit_bytes=60 * 2**20),
    )(*outs)
    return outs[:6] + tuple(v.reshape(H) for v in outs[6:])


def solution(mesh):
    in_specs = (
        P("seq", "head"),
        P("seq", "head"),
        P("head", "seq"),
        P(("seq", "head"), None),
        P(("seq", "head"), None),
        P("head"),
        P("head"),
        P("head"),
        P("seq", "head"),
    )
    out_specs = (
        P("seq", "head"),
        P("seq", "head"),
        P("seq", "head"),
        P("head", "seq"),
        P(("seq", "head"), None),
        P(("seq", "head"), None),
        P("head"),
        P("head"),
        P("head"),
    )
    return jax.shard_map(
        per_device, mesh=mesh, in_specs=in_specs, out_specs=out_specs, check_vma=False
    )
```

```python
import jax
import jax.numpy as jnp
from jax import lax
from jax.experimental import pallas as pl
from jax.experimental.pallas import tpu as pltpu
from jax.sharding import PartitionSpec as P

HEAD_DIM = 64
STATE = 256
GROUPS = 8
L = 128
NC = 8
H = 16
W = H * HEAD_DIM
ROWS = 64
F32, BF = jnp.float32, jnp.bfloat16
MESH = pl.DeviceIdType.MESH
HIGHEST = lax.Precision.HIGHEST
AROUND = (5, 4, 3, 2, 7, 6, 1)
LOG2E = 1.4426950408889634


def dot(a, b, ca, cb, precision=None):
    return lax.dot_general(
        a, b, (((ca,), (cb,)), ((), ())), preferred_element_type=F32, precision=precision
    )


def nn(a, b):
    return dot(a, b, 1, 0)


def nt(a, b):
    return dot(a, b, 1, 1)


def tn(a, b):
    return dot(a, b, 0, 0)


def remote(src, dst, send_sem, recv_sem, device):
    return pltpu.make_async_remote_copy(
        src_ref=src,
        dst_ref=dst,
        send_sem=send_sem,
        recv_sem=recv_sem,
        device_id=device,
        device_id_type=MESH,
    )


def repeat(first, last, body, times):
    def some(i, carry):
        for j in range(times):
            body(first + i * times + j, carry)
        return carry

    lax.fori_loop(0, (last - first) // times, some, 0)


def rows_of(index, count):
    return pl.ds(pl.multiple_of(index * count, count), count)


def kernel(
    x_hbm, z_hbm, g_hbm, dt_ref, b_hbm, c_hbm, alog_ref, bias_ref, skip_ref,
    gated_hbm, gx_hbm, gz_hbm, gdt_ref, gb_hbm, gc_hbm, galog_ref, gbias_ref, gskip_ref,
    x_v, z_v, g_v, xp, dy, xw, dyw, dtw, ecw, ww, e_s, dtv, ecv, wv, cumv, cumt,
    elw, prew, postw, skw, bc_v, s_loc, ds_loc, s_acc, yd, dxd, stage, sib, fin, gbc,
    sendf, sendg, recvf, recvg, outf, outg, s_in, ds_in, skipacc, fw, qs, ps, par,
    in_sem, out_sem, loc_sem, a_send, a_recv, f_send, f_recv, xf_send, xf_recv, xg_send, xg_recv,
    rf_send, rf_recv, rg_send, rg_recv, sib_send, sib_recv, fin_send, fin_recv, par_send, par_recv,
    gout_sem,
):
    seq = lax.axis_index("seq")
    hd = lax.axis_index("head")
    core = hd & 1
    chip = hd >> 1
    sibling = (seq, 2 * chip + 1 - core)

    def chip_at(k):
        return ((chip + k) & 3) | ((chip ^ k) & 4)

    def chip_back(k):
        return ((chip - k) & 3) | ((chip ^ k) & 4)

    def chip_dev(k):
        return (seq, 2 * chip_at(k) + core)

    def slab_at(k):
        return ((seq + (k & 6)) & 6) | ((seq ^ k) & 1)

    def slab_back(k):
        return ((seq - (k & 6)) & 6) | ((seq ^ k) & 1)

    def slab_dev(k):
        return (slab_at(k), hd)

    def load(a, c):
        src, dst = ((x_hbm, x_v), (z_hbm, z_v), (g_hbm, g_v))[a]
        return pltpu.make_async_copy(
            src.at[rows_of(c, L)], dst.at[rows_of(c, L)], in_sem.at[a, c]
        )

    def own_bc(t):
        src = (b_hbm, c_hbm)[t]
        return pltpu.make_async_copy(
            src.at[:, rows_of(chip, STATE)], bc_v.at[t, rows_of(hd, ROWS)], loc_sem.at[t]
        )

    for c in range(NC):
        for a in range(3):
            load(a, c).start()
    for t in range(2):
        own_bc(t).start()

    barrier = pltpu.get_barrier_semaphore()
    for k in range(1, NC):
        pl.semaphore_signal(barrier, inc=1, device_id=chip_dev(k), device_id_type=MESH)
        pl.semaphore_signal(barrier, inc=1, device_id=slab_dev(k), device_id_type=MESH)
    pl.semaphore_signal(barrier, inc=1, device_id=sibling, device_id_type=MESH)

    row16 = lax.broadcasted_iota(jnp.int32, (H, L), 0)

    def per_head(ref):
        column = jnp.zeros((H, L), F32)
        for h in range(H):
            column = jnp.where(row16 == h, ref[h], column)
        return jnp.concatenate([column] * NC, axis=0)

    rate = -jnp.exp(per_head(alog_ref))
    raw = dt_ref[...].astype(F32)
    pre = jnp.concatenate([raw[:, L * c : L * c + L] for c in range(NC)], axis=0) + per_head(bias_ref)
    step = jnp.maximum(pre, 0.0) + jnp.log1p(jnp.exp(-jnp.abs(pre)))
    decay = rate * step
    iota0 = lax.broadcasted_iota(jnp.int32, (L, L), 0)
    iota1 = lax.broadcasted_iota(jnp.int32, (L, L), 1)
    upper = (iota0 <= iota1).astype(F32)
    cum = dot(decay, upper, 1, 0, HIGHEST)
    ecum = jnp.exp(cum)
    tail = jnp.exp(cum[:, L - 1 : L] - cum)
    cum2 = cum * LOG2E
    cum_t = jnp.transpose(cum2)
    step_t = jnp.transpose(step)
    ecum_t = jnp.transpose(ecum)
    tail_t = jnp.transpose(tail)
    for c in range(NC):
        cumv[c] = cum2[H * c : H * c + H]
        cumt[c] = cum_t[:, H * c : H * c + H]
        for keep, value in ((dtv, step_t), (ecv, ecum_t), (wv, tail_t)):
            column = value[:, H * c : H * c + H]
            high = column.astype(BF)
            keep[c] = jnp.concatenate([high.astype(F32), column - high.astype(F32)], axis=1).astype(BF)
    head_of = lax.shift_right_logical(lax.broadcasted_iota(jnp.int32, (H, W), 1), 6)
    onehot = head_of == lax.broadcasted_iota(jnp.int32, (H, W), 0)
    spread_f = onehot.astype(F32)
    e_s[...] = jnp.concatenate([spread_f, spread_f], axis=0).astype(BF)
    last8 = jnp.concatenate([ecum_t[L - 1 : L, H * c : H * c + H] for c in range(NC)], axis=0)
    elast = dot(last8, spread_f, 1, 0, HIGHEST)
    skip_row = jnp.zeros((1, W), F32)
    for h in range(H):
        skip_row = jnp.where(head_of[0:1] == h, skip_ref[h], skip_row)
    skw[...] = skip_row
    run = jnp.ones((1, W), F32)
    for c in range(NC):
        elw[c] = elast[c : c + 1]
        prew[c] = run
        run = run * elast[c : c + 1]
    slab_decay = run
    run = jnp.ones((1, W), F32)
    for c in reversed(range(NC)):
        postw[c + 1] = run
        run = run * elast[c : c + 1]
    postw[0] = run
    skipacc[...] = jnp.zeros_like(skipacc)

    pl.semaphore_wait(barrier, 2 * NC - 1)

    def spread(t, k):
        src = (b_hbm, c_hbm)[t]
        device = sibling if k == 0 else chip_dev(k)
        group = chip if k == 0 else chip_at(k)
        return remote(
            src.at[:, rows_of(group, STATE)],
            bc_v.at[t, rows_of(hd, ROWS)],
            a_send.at[t, k],
            a_recv.at[t, k],
            device,
        )

    def arrived(t, k):
        place = 2 * chip + 1 - core if k == 0 else 2 * chip_back(k) + core
        return remote(
            b_hbm.at[:, rows_of(chip, STATE)],
            bc_v.at[t, rows_of(place, ROWS)],
            a_send.at[t, k],
            a_recv.at[t, k],
            sibling,
        )

    def forward(t, k, mine):
        place = 2 * chip_back(k) + (core if mine else 1 - core)
        block = bc_v.at[t, rows_of(place, ROWS)]
        return remote(block, block, f_send.at[t, k], f_recv.at[t, k], sibling)

    for t in range(2):
        for k in (6, 5, 7, 4, 2, 1, 3, 0):
            spread(t, k).start()

    def pass_on(t):
        for k in (4, 1, 3, 2, 5, 7, 6):
            arrived(t, k).wait_recv()
            forward(t, k, True).start()

    def complete(t):
        own_bc(t).wait()
        arrived(t, 0).wait_recv()
        for k in range(1, NC):
            forward(t, k, False).wait_recv()

    def prepare_x(c, carry):
        load(0, c).wait()
        r = rows_of(c, L)
        dt_c, w_c = dtv[c], wv[c]
        for p in range(W // 256):
            col = slice(256 * p, 256 * p + 256)
            e_c = e_s[:, col]
            dt_w, w_w = nn(dt_c, e_c), nn(w_c, e_c)
            dtw[r, col] = dt_w
            ww[r, col] = w_w
            scaled = x_v[r, col].astype(F32) * dt_w
            xp[r, col] = scaled.astype(BF)
            xw[r, col] = (scaled * w_w).astype(BF)
        return carry

    def prepare_g(c, carry):
        load(1, c).wait()
        load(2, c).wait()
        r = rows_of(c, L)
        ec_c = ecv[c]
        for p in range(W // 256):
            col = slice(256 * p, 256 * p + 256)
            ec_w = nn(ec_c, e_s[:, col])
            ecw[r, col] = ec_w
            x, z, g = (v[r, col].astype(F32) for v in (x_v, z_v, g_v))
            sig = 1.0 / (1.0 + jnp.exp(-z))
            silu = z * sig
            dy_f = g * silu
            dy[r, col] = dy_f.astype(BF)
            dyw[r, col] = (dy_f * ec_w).astype(BF)
            z_v[r, col] = silu.astype(BF)
            g_v[r, col] = (g * (sig + silu * (1.0 - sig))).astype(BF)
            skipacc[:, col] += jnp.sum((dy_f * x).reshape(L // 8, 8, 256), axis=0)
        return carry

    repeat(0, NC, prepare_x, 2)
    repeat(0, NC // 2, prepare_g, 2)
    pass_on(0)
    repeat(NC // 2, NC, prepare_g, 2)
    complete(0)

    def scan_state(first, keep, t, source, order):
        s_acc[...] = jnp.zeros_like(s_acc)

        def one(i, carry):
            c = order(i)
            r = rows_of(c, L)
            rows_t = jnp.transpose(bc_v[t, r, :])
            for p in range(W // 256):
                col = slice(256 * p, 256 * p + 256)
                now = s_acc[:, col]
                keep[c + first, :, col] = now.astype(BF)
                s_acc[:, col] = elw[c][:, col] * now + nn(rows_t, source[r, col])
            return carry

        repeat(0, NC, one, 4)

    def to_joiner(src, dst, send_sem, recv_sem, k):
        return remote(src.at[slab_at(k)], dst.at[seq], send_sem.at[k], recv_sem.at[k], slab_dev(k))

    def from_slab(src, dst, send_sem, recv_sem, k):
        place = slab_back(k)
        return remote(src.at[place], dst.at[place], send_sem.at[k], recv_sem.at[k], slab_dev(k))

    scan_state(0, s_loc, 0, xw, lambda i: i)
    high = slab_decay.astype(BF).astype(F32)
    decay_rows = jnp.concatenate(
        [high, slab_decay - high, jnp.zeros((14, W), F32)], axis=0
    ).astype(BF)
    for d in range(NC):
        col = slice(128 * d, 128 * d + 128)
        sendf[d, 0:STATE] = s_acc[:, col].astype(BF)
        sendf[d, STATE : STATE + 16] = decay_rows[:, col]
    @pl.when(seq != NC - 1)
    def _():
        for k in AROUND:
            to_joiner(sendf, recvf, xf_send, xf_recv, k).start()

    recvf[seq] = sendf[seq]

    pass_on(1)
    skip_sum = jnp.sum(dot(spread_f, skipacc[...], 1, 1, HIGHEST), axis=1, keepdims=True)
    complete(1)
    scan_state(1, ds_loc, 1, dyw, lambda i: NC - 1 - i)
    for p in range(W // 256):
        col = slice(256 * p, 256 * p + 256)
        ds_loc[0, :, col] = s_acc[:, col].astype(BF)
    for d in range(NC):
        sendg[d] = s_acc[:, 128 * d : 128 * d + 128].astype(BF)
    @pl.when(seq != 0)
    def _():
        for k in AROUND:
            to_joiner(sendg, recvg, xg_send, xg_recv, k).start()

    recvg[seq] = sendg[seq]

    low = iota0 >= iota1
    lane = lax.broadcasted_iota(jnp.int32, (1, L), 1)
    left = (lane < HEAD_DIM).astype(F32)
    left_b = left.astype(BF)
    right_b = (1.0 - left).astype(BF)

    def by_head(v, col):
        high = v.astype(BF)
        low_part = (v - high.astype(F32)).astype(BF)
        e_c = e_s[0:H, col]
        return nt(
            jnp.concatenate([e_c, e_c], axis=1), jnp.concatenate([high, low_part], axis=1)
        )

    def intra(c, carry):
        r = rows_of(c, L)
        b_c, c_c = bc_v[0, r, :], bc_v[1, r, :]
        scores = jnp.where(low, nt(c_c, b_c), 0.0)
        d_scores = jnp.zeros((L, L), F32)
        q = jnp.zeros((H, L), F32)
        px = jnp.zeros((H, L), F32)
        cum_r, cum_c = cumv[c], cumt[c]
        for p in range(H // 2):
            col = slice(L * p, L * p + L)
            x_p, dy_p = xp[r, col], dy[r, col]
            x_two = jnp.concatenate([x_p * left_b, x_p * right_b], axis=0)
            d_mix = nt(dy_p, x_two)
            parts = []
            for j in range(2):
                h = 2 * p + j
                seg = cum_c[:, h : h + 1] - cum_r[h : h + 1, :]
                mask = jnp.exp2(jnp.minimum(seg, 0.0))
                parts.append((scores * mask).astype(BF))
                d_scores = d_scores + d_mix[:, L * j : L * j + L] * mask
            mix = jnp.concatenate(parts, axis=1)
            y = nn(mix, x_two)
            yd[r, col] = y
            mix_t = jnp.concatenate([jnp.transpose(v) for v in parts], axis=1)
            dx = nn(mix_t, jnp.concatenate([dy_p * left_b, dy_p * right_b], axis=0))
            dxd[r, col] = dx
            p_x = x_p.astype(F32) * dx
            q = q + by_head(dy_p.astype(F32) * y - p_x, col)
            px = px + nt(e_s[0:H, col], p_x.astype(BF))
        d_scores = jnp.where(low, d_scores, 0.0).astype(BF)
        d_b = tn(d_scores, c_c)
        for p in range(W // 256):
            col = slice(256 * p, 256 * p + 256)
            d_b = d_b + nt(xw[r, col], ds_loc[c + 1, :, col])
        stage[c, 0] = d_b
        stage[c, 1] = nn(d_scores, b_c)
        qs[c] = q
        ps[c] = px
        return carry

    repeat(0, 2, intra, 2)

    def collect(src, dst, send_sem, recv_sem, absent):
        for k in range(1, NC):

            @pl.when(slab_back(k) != absent)
            def _():
                from_slab(src, dst, send_sem, recv_sem, k).wait_recv()

    collect(sendf, recvf, xf_send, xf_recv, NC - 1)
    run = jnp.zeros((STATE, L), F32)
    for i in range(NC):
        outf[i] = run.astype(BF)
        if i == 0:
            run = recvf[0, 0:STATE].astype(F32)
        elif i < NC - 1:
            factor = recvf[i, STATE : STATE + 16].astype(F32)
            run = (factor[0:1] + factor[1:2]) * run + recvf[i, 0:STATE].astype(F32)

    def back(src, dst, send_sem, recv_sem, k):
        return remote(
            src.at[slab_at(k)], dst.at[seq], send_sem.at[k], recv_sem.at[k], slab_dev(k)
        )

    def give_back(src, dst, send_sem, recv_sem, absent):
        for k in AROUND:

            @pl.when(slab_at(k) != absent)
            def _():
                back(src, dst, send_sem, recv_sem, k).start()

    give_back(outf, s_in, rf_send, rf_recv, 0)
    s_in[seq] = outf[seq]
    repeat(2, 6, intra, 2)
    collect(sendg, recvg, xg_send, xg_recv, 0)
    run = jnp.zeros((STATE, L), F32)
    for i in reversed(range(NC)):
        outg[i] = run.astype(BF)
        if i == NC - 1:
            run = recvg[i].astype(F32)
        elif i > 0:
            factor = recvf[i, STATE : STATE + 16].astype(F32)
            run = (factor[0:1] + factor[1:2]) * run + recvg[i].astype(F32)
    give_back(outg, ds_in, rg_send, rg_recv, NC - 1)
    ds_in[seq] = outg[seq]

    repeat(6, NC, intra, 2)

    def to_sibling(t, c):
        return remote(
            stage.at[c, t, rows_of(1 - core, ROWS)],
            sib.at[c, t],
            sib_send.at[t, c],
            sib_recv.at[t, c],
            sibling,
        )

    def to_owner(t, k):
        return remote(
            fin.at[chip_at(k), t],
            gbc.at[t, :, rows_of(chip, STATE)],
            fin_send.at[t, k],
            fin_recv.at[t, k],
            chip_dev(k),
        )

    def from_group(t, k):
        return remote(
            fin.at[chip_at(k), t],
            gbc.at[t, :, rows_of(chip_back(k), STATE)],
            fin_send.at[t, k],
            fin_recv.at[t, k],
            sibling,
        )

    def store(a, c):
        src, dst = ((x_v, gx_hbm), (z_v, gated_hbm), (g_v, gz_hbm))[a]
        return pltpu.make_async_copy(
            src.at[rows_of(c, L)], dst.at[rows_of(c, L)], out_sem.at[a, c]
        )

    def settle(t, k):
        c = chip_at(k)
        to_sibling(t, c).wait_recv()
        total = (stage[c, t, rows_of(core, ROWS)] + sib[c, t]).astype(BF)

        @pl.when(k == 0)
        def _():
            gbc[t, :, rows_of(chip, STATE)] = total

        @pl.when(k > 0)
        def _():
            fin[c, t] = total
            to_owner(t, k).start()

    def finish_y(k, carry):
        c = chip_at(k)
        r = rows_of(c, L)
        c_c = bc_v[1, r, :]
        d_c = stage[c, 1]
        q = jnp.zeros((H, L), F32)

        def states(p):
            col = slice(256 * p, 256 * p + 256)
            start = jnp.concatenate([s_in[2 * p], s_in[2 * p + 1]], axis=1).astype(F32)
            s_b = (s_loc[c, :, col].astype(F32) + prew[c][:, col] * start).astype(BF)
            s_loc[c, :, col] = s_b
            return nt(dyw[r, col], s_b), nn(c_c, s_b)

        ahead = states(0)
        for p in range(W // 256):
            col = slice(256 * p, 256 * p + 256)
            now = ahead
            if p + 1 < W // 256:
                ahead = states(p + 1)
            d_c = d_c + now[0]
            off = ecw[r, col] * now[1]
            q = q + nt(e_s[0:H, col], (dy[r, col].astype(F32) * off).astype(BF))
            y = yd[r, col] + off + skw[:, col] * x_v[r, col].astype(F32)
            z_v[r, col] = (y * z_v[r, col].astype(F32)).astype(BF)
            g_v[r, col] = (y * g_v[r, col].astype(F32)).astype(BF)
        stage[c, 1] = d_c
        qs[c] += q
        store(1, c).start()
        store(2, c).start()
        to_sibling(1, c).start()

        @pl.when(k >= 2)
        def _():
            settle(1, k - 2)

        return carry

    def two(p):
        return jnp.concatenate([ds_in[2 * p], ds_in[2 * p + 1]], axis=1)

    def finish_b(m, carry):
        d_b = jnp.zeros((2 * L, STATE), F32)
        for p in range(W // 256):
            col = slice(256 * p, 256 * p + 256)
            scaled = [
                (xw[rows_of(c, L), col].astype(F32) * postw[c + 1][:, col]).astype(BF)
                for c in (2 * m, 2 * m + 1)
            ]
            d_b = d_b + nt(jnp.concatenate(scaled, axis=0), two(p))
        for j in range(2):
            stage[2 * m + j, 0] += d_b[L * j : L * j + L]
            to_sibling(0, 2 * m + j).start()
        return carry

    def whole(c, p):
        col = slice(256 * p, 256 * p + 256)
        ds_t = ds_loc[c, :, col].astype(F32) + postw[c][:, col] * two(p).astype(F32)
        ds_loc[c, :, col] = ds_t.astype(BF)

    def finish_x(c, carry):
        r = rows_of(c, L)
        b_c = bc_v[0, r, :]
        px = jnp.zeros((H, L), F32)
        for p in range(W // 256):
            col = slice(256 * p, 256 * p + 256)
            whole(c + 1, p)
            off = ww[r, col] * nn(b_c, ds_loc[c + 1, :, col])
            px = px + nt(e_s[0:H, col], (xp[r, col].astype(F32) * off).astype(BF))
            dx = dxd[r, col] + off
            x_v[r, col] = (skw[:, col] * dy[r, col].astype(F32) + dtw[r, col] * dx).astype(BF)
            pair = s_loc[c, :, col].astype(F32) * ds_loc[c, :, col].astype(F32)
            fw[c, :, col] = jnp.sum(pair, axis=0, keepdims=True)
        ps[c] += px
        qs[c] -= px
        store(0, c).start()
        return carry

    def settle_from(t, first):
        def one(k, carry):
            settle(t, k)
            return carry

        lax.fori_loop(first, NC, one, 0)

    @pl.when(seq == 0)
    def _():
        s_in[...] = jnp.zeros_like(s_in)

    @pl.when(seq != 0)
    def _():
        for k in range(1, NC):
            from_slab(outf, s_in, rf_send, rf_recv, k).wait_recv()

    repeat(0, NC, finish_y, 2)
    settle_from(1, NC - 2)

    @pl.when(seq == NC - 1)
    def _():
        ds_in[...] = jnp.zeros_like(ds_in)

    @pl.when(seq != NC - 1)
    def _():
        for k in range(1, NC):
            from_slab(outg, ds_in, rg_send, rg_recv, k).wait_recv()

    lax.fori_loop(0, NC // 2, finish_b, 0)
    for p in range(W // 256):
        whole(0, p)
    repeat(0, 2, finish_x, 2)
    settle_from(0, 0)
    repeat(2, NC, finish_x, 2)

    q = qs[...].reshape(L, L)
    px = ps[...].reshape(L, L)
    before = dot(q, (iota0 < iota1).astype(F32), 1, 0, HIGHEST)
    pairs = dot(spread_f, fw[...].reshape(NC, W), 1, 1, HIGHEST)
    boundary = jnp.concatenate([pairs[:, c : c + 1] for c in range(NC)], axis=0)
    d_decay = boundary - before
    d_step = px / step + rate * d_decay
    d_raw = d_step / (1.0 + jnp.exp(-pre))
    for c in range(NC):
        gdt_ref[:, L * c : L * c + L] = d_raw[H * c : H * c + H].astype(BF)

    def over_tokens(v):
        column = jnp.sum(v, axis=1, keepdims=True)
        total = column[0:H]
        for c in range(1, NC):
            total = total + column[H * c : H * c + H]
        return total

    lane16 = lax.broadcasted_iota(jnp.int32, (H, L), 1)
    par[0] = jnp.where(
        lane16 == 0,
        over_tokens(d_decay * decay),
        jnp.where(lane16 == 1, over_tokens(d_raw), skip_sum),
    )

    def share(k):
        return remote(par.at[0], par.at[k], par_send.at[k], par_recv.at[k], slab_dev(k))

    for k in range(1, NC):
        share(k).start()
    for k in range(1, NC):
        for t in range(2):
            from_group(t, k).wait_recv()
    outs = [
        pltpu.make_async_copy(gbc.at[0], gb_hbm, gout_sem.at[0]),
        pltpu.make_async_copy(gbc.at[1], gc_hbm, gout_sem.at[1]),
    ]
    for o in outs:
        o.start()
    for k in range(1, NC):
        share(k).wait_recv()
    total = par[0]
    for k in range(1, NC):
        total = total + par[k]
    flat = jnp.transpose(jnp.concatenate([total] * NC, axis=0))
    galog_ref[...] = flat[0:1, 0:H]
    gbias_ref[...] = flat[1:2, 0:H]
    gskip_ref[...] = flat[2:3, 0:H]

    for o in outs:
        o.wait()
    for k in range(NC):
        for t in range(2):
            spread(t, k).wait_send()
            to_sibling(t, k).wait_send()
    for k in range(1, NC):
        for t in range(2):
            forward(t, k, True).wait_send()
            to_owner(t, k).wait_send()

        @pl.when(seq != NC - 1)
        def _():
            to_joiner(sendf, recvf, xf_send, xf_recv, k).wait_send()

        @pl.when(seq != 0)
        def _():
            to_joiner(sendg, recvg, xg_send, xg_recv, k).wait_send()

        @pl.when(slab_at(k) != 0)
        def _():
            back(outf, s_in, rf_send, rf_recv, k).wait_send()

        @pl.when(slab_at(k) != NC - 1)
        def _():
            back(outg, ds_in, rg_send, rg_recv, k).wait_send()

        share(k).wait_send()
    for c in range(NC):
        for a in range(3):
            store(a, c).wait()


def hand_out(*refs):
    ins, outs, held, (in_sem, out_sem) = refs[:9], refs[9:18], refs[18:27], refs[27:]
    blocks = [(a, pl.ds(L * c, L), NC * a + c) for c in range(NC) for a in range(3)]
    blocks += [(a, slice(None), 3 * NC + a - 3) for a in range(3, 9)]
    loads = [pltpu.make_async_copy(ins[a].at[r], held[a].at[r], in_sem.at[s]) for a, r, s in blocks]
    stores = [pltpu.make_async_copy(held[a].at[r], outs[a].at[r], out_sem.at[s]) for a, r, s in blocks]
    for load in loads:
        load.start()
    for load, store in zip(loads, stores):
        load.wait()
        store.start()
    for store in stores:
        store.wait()


def per_device(inner_x, gate_z, dt_raw, b_proj, c_proj, a_log, dt_bias, d_skip, grad_gated):
    tokens = inner_x.shape[0]
    any_space = pl.BlockSpec(memory_space=pl.ANY)
    vmem = pl.BlockSpec(memory_space=pltpu.VMEM)
    smem = pl.BlockSpec(memory_space=pltpu.SMEM)
    sem = pltpu.SemaphoreType.DMA
    big = jax.ShapeDtypeStruct((tokens, W), BF)
    rows = jax.ShapeDtypeStruct((ROWS, GROUPS * STATE), BF)
    head = jax.ShapeDtypeStruct((1, H), F32)
    wide = pltpu.VMEM((tokens, W), BF)
    wide_f = pltpu.VMEM((tokens, W), F32)
    scratch = [
        wide, wide, wide,
        wide, wide, wide, wide,
        wide_f, wide_f, wide_f,
        pltpu.VMEM((2 * H, W), BF),
        pltpu.VMEM((NC, L, 2 * H), BF),
        pltpu.VMEM((NC, L, 2 * H), BF),
        pltpu.VMEM((NC, L, 2 * H), BF),
        pltpu.VMEM((NC, H, L), F32),
        pltpu.VMEM((NC, L, H), F32),
        pltpu.VMEM((NC, 1, W), F32),
        pltpu.VMEM((NC, 1, W), F32),
        pltpu.VMEM((NC + 1, 1, W), F32),
        pltpu.VMEM((1, W), F32),
        pltpu.VMEM((2, tokens, STATE), BF),
        pltpu.VMEM((NC, STATE, W), BF),
        pltpu.VMEM((NC + 1, STATE, W), BF),
        pltpu.VMEM((STATE, W), F32),
        pltpu.VMEM((tokens, W), F32),
        pltpu.VMEM((tokens, W), F32),
        pltpu.VMEM((NC, 2, L, STATE), F32),
        pltpu.VMEM((NC, 2, ROWS, STATE), F32),
        pltpu.VMEM((NC, 2, ROWS, STATE), BF),
        pltpu.VMEM((2, ROWS, GROUPS * STATE), BF),
        pltpu.VMEM((NC, STATE + 16, L), BF),
        pltpu.VMEM((NC, STATE, L), BF),
        pltpu.VMEM((NC, STATE + 16, L), BF),
        pltpu.VMEM((NC, STATE, L), BF),
        pltpu.VMEM((NC, STATE, L), BF),
        pltpu.VMEM((NC, STATE, L), BF),
        pltpu.VMEM((NC, STATE, L), BF),
        pltpu.VMEM((NC, STATE, L), BF),
        pltpu.VMEM((8, W), F32),
        pltpu.VMEM((NC, 1, W), F32),
        pltpu.VMEM((NC, H, L), F32),
        pltpu.VMEM((NC, H, L), F32),
        pltpu.VMEM((NC, H, L), F32),
        sem((3, NC)), sem((3, NC)), sem((2,)),
        sem((2, NC)), sem((2, NC)), sem((2, NC)), sem((2, NC)),
        sem((NC,)), sem((NC,)), sem((NC,)), sem((NC,)),
        sem((NC,)), sem((NC,)), sem((NC,)), sem((NC,)),
        sem((2, NC)), sem((2, NC)), sem((2, NC)), sem((2, NC)), sem((NC,)), sem((NC,)),
        sem((2,)),
    ]
    small = (jax.ShapeDtypeStruct((H, tokens), BF), rows, rows, head, head, head)
    outs = pl.pallas_call(
        kernel,
        out_shape=(big, big, big) + small,
        in_specs=[any_space, any_space, any_space, vmem, any_space, any_space, smem, smem, smem],
        out_specs=(any_space, any_space, any_space, vmem, any_space, any_space, vmem, vmem, vmem),
        scratch_shapes=scratch,
        compiler_params=pltpu.CompilerParams(
            collective_id=0, has_side_effects=True, vmem_limit_bytes=60 * 2**20
        ),
    )(inner_x, gate_z, grad_gated, dt_raw, b_proj, c_proj, a_log, dt_bias, d_skip)
    outs = pl.pallas_call(
        hand_out,
        out_shape=(big, big, big) + small,
        in_specs=[any_space] * 9,
        out_specs=(any_space,) * 9,
        scratch_shapes=[pltpu.VMEM(v.shape, v.dtype) for v in outs]
        + [sem((3 * NC + 6,)), sem((3 * NC + 6,))],
        compiler_params=pltpu.CompilerParams(vmem_limit_bytes=60 * 2**20),
    )(*outs)
    return outs[:6] + tuple(v.reshape(H) for v in outs[6:])


def solution(mesh):
    in_specs = (
        P("seq", "head"),
        P("seq", "head"),
        P("head", "seq"),
        P(("seq", "head"), None),
        P(("seq", "head"), None),
        P("head"),
        P("head"),
        P("head"),
        P("seq", "head"),
    )
    out_specs = (
        P("seq", "head"),
        P("seq", "head"),
        P("seq", "head"),
        P("head", "seq"),
        P(("seq", "head"), None),
        P(("seq", "head"), None),
        P("head"),
        P("head"),
        P("head"),
    )
    return jax.shard_map(
        per_device, mesh=mesh, in_specs=in_specs, out_specs=out_specs, check_vma=False
    )
```

```python
import jax
import jax.numpy as jnp
from jax import lax
from jax.experimental import pallas as pl
from jax.experimental.pallas import tpu as pltpu
from jax.sharding import PartitionSpec as P

HEAD_DIM = 64
STATE = 256
GROUPS = 8
L = 128
NC = 8
H = 16
W = H * HEAD_DIM
ROWS = 64
F32, BF = jnp.float32, jnp.bfloat16
MESH = pl.DeviceIdType.MESH
HIGHEST = lax.Precision.HIGHEST
AROUND = (5, 4, 3, 2, 7, 6, 1)
LOG2E = 1.4426950408889634


def dot(a, b, ca, cb, precision=None):
    return lax.dot_general(
        a, b, (((ca,), (cb,)), ((), ())), preferred_element_type=F32, precision=precision
    )


def nn(a, b):
    return dot(a, b, 1, 0)


def nt(a, b):
    return dot(a, b, 1, 1)


def tn(a, b):
    return dot(a, b, 0, 0)


def remote(src, dst, send_sem, recv_sem, device):
    return pltpu.make_async_remote_copy(
        src_ref=src,
        dst_ref=dst,
        send_sem=send_sem,
        recv_sem=recv_sem,
        device_id=device,
        device_id_type=MESH,
    )


def repeat(first, last, body, times):
    def some(i, carry):
        for j in range(times):
            body(first + i * times + j, carry)
        return carry

    lax.fori_loop(0, (last - first) // times, some, 0)


def rows_of(index, count):
    return pl.ds(pl.multiple_of(index * count, count), count)


def kernel(
    x_hbm, z_hbm, g_hbm, dt_ref, b_hbm, c_hbm, alog_ref, bias_ref, skip_ref,
    gated_hbm, gx_hbm, gz_hbm, gdt_ref, gb_hbm, gc_hbm, galog_ref, gbias_ref, gskip_ref,
    x_v, z_v, g_v, xp, dy, xw, dyw, dtw, ecw, ww, e_s, dtv, ecv, wv, cumv, cumt,
    elw, prew, postw, skw, bc_v, s_loc, ds_loc, s_acc, yd, dxd, stage, sib, fin, gbc,
    sendf, sendg, recvf, recvg, outf, outg, s_in, ds_in, skipacc, fw, qs, ps, par,
    in_sem, out_sem, loc_sem, a_send, a_recv, f_send, f_recv, xf_send, xf_recv, xg_send, xg_recv,
    rf_send, rf_recv, rg_send, rg_recv, sib_send, sib_recv, fin_send, fin_recv, par_send, par_recv,
    gout_sem,
):
    seq = lax.axis_index("seq")
    hd = lax.axis_index("head")
    core = hd & 1
    chip = hd >> 1
    sibling = (seq, 2 * chip + 1 - core)

    def chip_at(k):
        return ((chip + k) & 3) | ((chip ^ k) & 4)

    def chip_back(k):
        return ((chip - k) & 3) | ((chip ^ k) & 4)

    def chip_dev(k):
        return (seq, 2 * chip_at(k) + core)

    def slab_at(k):
        return ((seq + (k & 6)) & 6) | ((seq ^ k) & 1)

    def slab_back(k):
        return ((seq - (k & 6)) & 6) | ((seq ^ k) & 1)

    def slab_dev(k):
        return (slab_at(k), hd)

    def load(a, c):
        src, dst = ((x_hbm, x_v), (z_hbm, z_v), (g_hbm, g_v))[a]
        return pltpu.make_async_copy(
            src.at[rows_of(c, L)], dst.at[rows_of(c, L)], in_sem.at[a, c]
        )

    def own_bc(t):
        src = (b_hbm, c_hbm)[t]
        return pltpu.make_async_copy(
            src.at[:, rows_of(chip, STATE)], bc_v.at[t, rows_of(hd, ROWS)], loc_sem.at[t]
        )

    for c in range(NC):
        load(0, c).start()

    barrier = pltpu.get_barrier_semaphore()
    for k in range(1, NC):
        pl.semaphore_signal(barrier, inc=1, device_id=chip_dev(k), device_id_type=MESH)
        pl.semaphore_signal(barrier, inc=1, device_id=slab_dev(k), device_id_type=MESH)
    pl.semaphore_signal(barrier, inc=1, device_id=sibling, device_id_type=MESH)

    row16 = lax.broadcasted_iota(jnp.int32, (H, L), 0)

    def per_head(ref):
        column = jnp.zeros((H, L), F32)
        for h in range(H):
            column = jnp.where(row16 == h, ref[h], column)
        return jnp.concatenate([column] * NC, axis=0)

    rate = -jnp.exp(per_head(alog_ref))
    raw = dt_ref[...].astype(F32)
    pre = jnp.concatenate([raw[:, L * c : L * c + L] for c in range(NC)], axis=0) + per_head(bias_ref)
    step = jnp.maximum(pre, 0.0) + jnp.log1p(jnp.exp(-jnp.abs(pre)))
    decay = rate * step
    iota0 = lax.broadcasted_iota(jnp.int32, (L, L), 0)
    iota1 = lax.broadcasted_iota(jnp.int32, (L, L), 1)
    upper = (iota0 <= iota1).astype(F32)
    cum = dot(decay, upper, 1, 0, HIGHEST)
    ecum = jnp.exp(cum)
    tail = jnp.exp(cum[:, L - 1 : L] - cum)
    cum2 = cum * LOG2E
    cum_t = jnp.transpose(cum2)
    step_t = jnp.transpose(step)
    ecum_t = jnp.transpose(ecum)
    tail_t = jnp.transpose(tail)
    for c in range(NC):
        cumv[c] = cum2[H * c : H * c + H]
        cumt[c] = cum_t[:, H * c : H * c + H]
        for keep, value in ((dtv, step_t), (ecv, ecum_t), (wv, tail_t)):
            column = value[:, H * c : H * c + H]
            high = column.astype(BF)
            keep[c] = jnp.concatenate([high.astype(F32), column - high.astype(F32)], axis=1).astype(BF)
    head_of = lax.shift_right_logical(lax.broadcasted_iota(jnp.int32, (H, W), 1), 6)
    onehot = head_of == lax.broadcasted_iota(jnp.int32, (H, W), 0)
    spread_f = onehot.astype(F32)
    e_s[...] = jnp.concatenate([spread_f, spread_f], axis=0).astype(BF)
    last8 = jnp.concatenate([ecum_t[L - 1 : L, H * c : H * c + H] for c in range(NC)], axis=0)
    elast = dot(last8, spread_f, 1, 0, HIGHEST)
    skip_row = jnp.zeros((1, W), F32)
    for h in range(H):
        skip_row = jnp.where(head_of[0:1] == h, skip_ref[h], skip_row)
    skw[...] = skip_row
    run = jnp.ones((1, W), F32)
    for c in range(NC):
        elw[c] = elast[c : c + 1]
        prew[c] = run
        run = run * elast[c : c + 1]
    slab_decay = run
    run = jnp.ones((1, W), F32)
    for c in reversed(range(NC)):
        postw[c + 1] = run
        run = run * elast[c : c + 1]
    postw[0] = run
    skipacc[...] = jnp.zeros_like(skipacc)

    pl.semaphore_wait(barrier, 2 * NC - 1)

    def spread(t, k):
        src = (b_hbm, c_hbm)[t]
        device = sibling if k == 0 else chip_dev(k)
        group = chip if k == 0 else chip_at(k)
        return remote(
            src.at[:, rows_of(group, STATE)],
            bc_v.at[t, rows_of(hd, ROWS)],
            a_send.at[t, k],
            a_recv.at[t, k],
            device,
        )

    def arrived(t, k):
        place = 2 * chip + 1 - core if k == 0 else 2 * chip_back(k) + core
        return remote(
            b_hbm.at[:, rows_of(chip, STATE)],
            bc_v.at[t, rows_of(place, ROWS)],
            a_send.at[t, k],
            a_recv.at[t, k],
            sibling,
        )

    def forward(t, k, mine):
        place = 2 * chip_back(k) + (core if mine else 1 - core)
        block = bc_v.at[t, rows_of(place, ROWS)]
        return remote(block, block, f_send.at[t, k], f_recv.at[t, k], sibling)

    for t in range(2):
        for k in (6, 5, 7, 4, 2, 1, 3, 0):
            spread(t, k).start()
        own_bc(t).start()
    for c in range(NC):
        load(1, c).start()
        load(2, c).start()

    def pass_on(t):
        for k in (4, 1, 3, 2, 5, 7, 6):
            arrived(t, k).wait_recv()
            forward(t, k, True).start()

    def complete(t):
        own_bc(t).wait()
        arrived(t, 0).wait_recv()
        for k in range(1, NC):
            forward(t, k, False).wait_recv()

    def prepare_x(c, carry):
        load(0, c).wait()
        r = rows_of(c, L)
        dt_c, w_c = dtv[c], wv[c]
        for p in range(W // 256):
            col = slice(256 * p, 256 * p + 256)
            e_c = e_s[:, col]
            dt_w, w_w = nn(dt_c, e_c), nn(w_c, e_c)
            dtw[r, col] = dt_w
            ww[r, col] = w_w
            scaled = x_v[r, col].astype(F32) * dt_w
            xp[r, col] = scaled.astype(BF)
            xw[r, col] = (scaled * w_w).astype(BF)
        return carry

    def prepare_g(c, carry):
        load(1, c).wait()
        load(2, c).wait()
        r = rows_of(c, L)
        ec_c = ecv[c]
        for p in range(W // 256):
            col = slice(256 * p, 256 * p + 256)
            ec_w = nn(ec_c, e_s[:, col])
            ecw[r, col] = ec_w
            x, z, g = (v[r, col].astype(F32) for v in (x_v, z_v, g_v))
            sig = 1.0 / (1.0 + jnp.exp(-z))
            silu = z * sig
            dy_f = g * silu
            dy[r, col] = dy_f.astype(BF)
            dyw[r, col] = (dy_f * ec_w).astype(BF)
            z_v[r, col] = silu.astype(BF)
            g_v[r, col] = (g * (sig + silu * (1.0 - sig))).astype(BF)
            skipacc[:, col] += jnp.sum((dy_f * x).reshape(L // 8, 8, 256), axis=0)
        return carry

    repeat(0, NC, prepare_x, 2)
    pass_on(0)
    complete(0)

    def scan_state(first, keep, t, source, order):
        s_acc[...] = jnp.zeros_like(s_acc)

        def one(i, carry):
            c = order(i)
            r = rows_of(c, L)
            rows_t = jnp.transpose(bc_v[t, r, :])
            for p in range(W // 256):
                col = slice(256 * p, 256 * p + 256)
                now = s_acc[:, col]
                keep[c + first, :, col] = now.astype(BF)
                s_acc[:, col] = elw[c][:, col] * now + nn(rows_t, source[r, col])
            return carry

        repeat(0, NC, one, 4)

    def to_joiner(src, dst, send_sem, recv_sem, k):
        return remote(src.at[slab_at(k)], dst.at[seq], send_sem.at[k], recv_sem.at[k], slab_dev(k))

    def from_slab(src, dst, send_sem, recv_sem, k):
        place = slab_back(k)
        return remote(src.at[place], dst.at[place], send_sem.at[k], recv_sem.at[k], slab_dev(k))

    scan_state(0, s_loc, 0, xw, lambda i: i)
    high = slab_decay.astype(BF).astype(F32)
    decay_rows = jnp.concatenate(
        [high, slab_decay - high, jnp.zeros((14, W), F32)], axis=0
    ).astype(BF)
    for d in range(NC):
        col = slice(128 * d, 128 * d + 128)
        sendf[d, 0:STATE] = s_acc[:, col].astype(BF)
        sendf[d, STATE : STATE + 16] = decay_rows[:, col]
    @pl.when(seq != NC - 1)
    def _():
        for k in AROUND:
            to_joiner(sendf, recvf, xf_send, xf_recv, k).start()

    recvf[seq] = sendf[seq]

    pass_on(1)
    repeat(0, NC, prepare_g, 2)
    skip_sum = jnp.sum(dot(spread_f, skipacc[...], 1, 1, HIGHEST), axis=1, keepdims=True)
    complete(1)
    scan_state(1, ds_loc, 1, dyw, lambda i: NC - 1 - i)
    for p in range(W // 256):
        col = slice(256 * p, 256 * p + 256)
        ds_loc[0, :, col] = s_acc[:, col].astype(BF)
    for d in range(NC):
        sendg[d] = s_acc[:, 128 * d : 128 * d + 128].astype(BF)
    @pl.when(seq != 0)
    def _():
        for k in AROUND:
            to_joiner(sendg, recvg, xg_send, xg_recv, k).start()

    recvg[seq] = sendg[seq]

    low = iota0 >= iota1
    lane = lax.broadcasted_iota(jnp.int32, (1, L), 1)
    left = (lane < HEAD_DIM).astype(F32)
    left_b = left.astype(BF)
    right_b = (1.0 - left).astype(BF)

    def by_head(v, col):
        high = v.astype(BF)
        low_part = (v - high.astype(F32)).astype(BF)
        e_c = e_s[0:H, col]
        return nt(
            jnp.concatenate([e_c, e_c], axis=1), jnp.concatenate([high, low_part], axis=1)
        )

    def intra(c, carry):
        r = rows_of(c, L)
        b_c, c_c = bc_v[0, r, :], bc_v[1, r, :]
        scores = jnp.where(low, nt(c_c, b_c), 0.0)
        d_scores = jnp.zeros((L, L), F32)
        q = jnp.zeros((H, L), F32)
        px = jnp.zeros((H, L), F32)
        cum_r, cum_c = cumv[c], cumt[c]
        for p in range(H // 2):
            col = slice(L * p, L * p + L)
            x_p, dy_p = xp[r, col], dy[r, col]
            x_two = jnp.concatenate([x_p * left_b, x_p * right_b], axis=0)
            d_mix = nt(dy_p, x_two)
            parts = []
            for j in range(2):
                h = 2 * p + j
                seg = cum_c[:, h : h + 1] - cum_r[h : h + 1, :]
                mask = jnp.exp2(jnp.minimum(seg, 0.0))
                parts.append((scores * mask).astype(BF))
                d_scores = d_scores + d_mix[:, L * j : L * j + L] * mask
            mix = jnp.concatenate(parts, axis=1)
            y = nn(mix, x_two)
            yd[r, col] = y
            mix_t = jnp.concatenate([jnp.transpose(v) for v in parts], axis=1)
            dx = nn(mix_t, jnp.concatenate([dy_p * left_b, dy_p * right_b], axis=0))
            dxd[r, col] = dx
            p_x = x_p.astype(F32) * dx
            q = q + by_head(dy_p.astype(F32) * y - p_x, col)
            px = px + nt(e_s[0:H, col], p_x.astype(BF))
        d_scores = jnp.where(low, d_scores, 0.0).astype(BF)
        d_b = tn(d_scores, c_c)
        for p in range(W // 256):
            col = slice(256 * p, 256 * p + 256)
            d_b = d_b + nt(xw[r, col], ds_loc[c + 1, :, col])
        stage[c, 0] = d_b
        stage[c, 1] = nn(d_scores, b_c)
        qs[c] = q
        ps[c] = px
        return carry

    repeat(0, 2, intra, 2)

    def collect(src, dst, send_sem, recv_sem, absent):
        for k in range(1, NC):

            @pl.when(slab_back(k) != absent)
            def _():
                from_slab(src, dst, send_sem, recv_sem, k).wait_recv()

    collect(sendf, recvf, xf_send, xf_recv, NC - 1)
    run = jnp.zeros((STATE, L), F32)
    for i in range(NC):
        outf[i] = run.astype(BF)
        if i == 0:
            run = recvf[0, 0:STATE].astype(F32)
        elif i < NC - 1:
            factor = recvf[i, STATE : STATE + 16].astype(F32)
            run = (factor[0:1] + factor[1:2]) * run + recvf[i, 0:STATE].astype(F32)

    def back(src, dst, send_sem, recv_sem, k):
        return remote(
            src.at[slab_at(k)], dst.at[seq], send_sem.at[k], recv_sem.at[k], slab_dev(k)
        )

    def give_back(src, dst, send_sem, recv_sem, absent):
        for k in AROUND:

            @pl.when(slab_at(k) != absent)
            def _():
                back(src, dst, send_sem, recv_sem, k).start()

    give_back(outf, s_in, rf_send, rf_recv, 0)
    s_in[seq] = outf[seq]
    repeat(2, 6, intra, 4)
    collect(sendg, recvg, xg_send, xg_recv, 0)
    run = jnp.zeros((STATE, L), F32)
    for i in reversed(range(NC)):
        outg[i] = run.astype(BF)
        if i == NC - 1:
            run = recvg[i].astype(F32)
        elif i > 0:
            factor = recvf[i, STATE : STATE + 16].astype(F32)
            run = (factor[0:1] + factor[1:2]) * run + recvg[i].astype(F32)
    give_back(outg, ds_in, rg_send, rg_recv, NC - 1)
    ds_in[seq] = outg[seq]

    repeat(6, NC, intra, 2)

    def to_sibling(t, c):
        return remote(
            stage.at[c, t, rows_of(1 - core, ROWS)],
            sib.at[c, t],
            sib_send.at[t, c],
            sib_recv.at[t, c],
            sibling,
        )

    def to_owner(t, k):
        return remote(
            fin.at[chip_at(k), t],
            gbc.at[t, :, rows_of(chip, STATE)],
            fin_send.at[t, k],
            fin_recv.at[t, k],
            chip_dev(k),
        )

    def from_group(t, k):
        return remote(
            fin.at[chip_at(k), t],
            gbc.at[t, :, rows_of(chip_back(k), STATE)],
            fin_send.at[t, k],
            fin_recv.at[t, k],
            sibling,
        )

    def store(a, c):
        src, dst = ((x_v, gx_hbm), (z_v, gated_hbm), (g_v, gz_hbm))[a]
        return pltpu.make_async_copy(
            src.at[rows_of(c, L)], dst.at[rows_of(c, L)], out_sem.at[a, c]
        )

    def settle(t, k):
        c = chip_at(k)
        to_sibling(t, c).wait_recv()
        total = (stage[c, t, rows_of(core, ROWS)] + sib[c, t]).astype(BF)

        @pl.when(k == 0)
        def _():
            gbc[t, :, rows_of(chip, STATE)] = total

        @pl.when(k > 0)
        def _():
            fin[c, t] = total
            to_owner(t, k).start()

    def finish_y(k, carry):
        c = chip_at(k)
        r = rows_of(c, L)
        c_c = bc_v[1, r, :]
        d_c = stage[c, 1]
        q = jnp.zeros((H, L), F32)

        def states(p):
            col = slice(256 * p, 256 * p + 256)
            start = jnp.concatenate([s_in[2 * p], s_in[2 * p + 1]], axis=1).astype(F32)
            s_b = (s_loc[c, :, col].astype(F32) + prew[c][:, col] * start).astype(BF)
            s_loc[c, :, col] = s_b
            return nt(dyw[r, col], s_b), nn(c_c, s_b)

        ahead = states(0)
        for p in range(W // 256):
            col = slice(256 * p, 256 * p + 256)
            now = ahead
            if p + 1 < W // 256:
                ahead = states(p + 1)
            d_c = d_c + now[0]
            off = ecw[r, col] * now[1]
            q = q + nt(e_s[0:H, col], (dy[r, col].astype(F32) * off).astype(BF))
            y = yd[r, col] + off + skw[:, col] * x_v[r, col].astype(F32)
            z_v[r, col] = (y * z_v[r, col].astype(F32)).astype(BF)
            g_v[r, col] = (y * g_v[r, col].astype(F32)).astype(BF)
        stage[c, 1] = d_c
        qs[c] += q
        store(1, c).start()
        store(2, c).start()
        to_sibling(1, c).start()

        @pl.when(k >= 2)
        def _():
            settle(1, k - 2)

        return carry

    def two(p):
        return jnp.concatenate([ds_in[2 * p], ds_in[2 * p + 1]], axis=1)

    def finish_b(m, carry):
        d_b = jnp.zeros((2 * L, STATE), F32)
        for p in range(W // 256):
            col = slice(256 * p, 256 * p + 256)
            scaled = [
                (xw[rows_of(c, L), col].astype(F32) * postw[c + 1][:, col]).astype(BF)
                for c in (2 * m, 2 * m + 1)
            ]
            d_b = d_b + nt(jnp.concatenate(scaled, axis=0), two(p))
        for j in range(2):
            stage[2 * m + j, 0] += d_b[L * j : L * j + L]
            to_sibling(0, 2 * m + j).start()
        return carry

    def whole(c, p):
        col = slice(256 * p, 256 * p + 256)
        ds_t = ds_loc[c, :, col].astype(F32) + postw[c][:, col] * two(p).astype(F32)
        ds_loc[c, :, col] = ds_t.astype(BF)

    def finish_x(c, carry):
        r = rows_of(c, L)
        b_c = bc_v[0, r, :]
        px = jnp.zeros((H, L), F32)
        for p in range(W // 256):
            col = slice(256 * p, 256 * p + 256)
            whole(c + 1, p)
            off = ww[r, col] * nn(b_c, ds_loc[c + 1, :, col])
            px = px + nt(e_s[0:H, col], (xp[r, col].astype(F32) * off).astype(BF))
            dxd[r, col] += off
            pair = s_loc[c, :, col].astype(F32) * ds_loc[c, :, col].astype(F32)
            fw[c, :, col] = jnp.sum(pair, axis=0, keepdims=True)
        ps[c] += px
        qs[c] -= px
        return carry

    def finish_gx(c, carry):
        r = rows_of(c, L)
        for p in range(W // 256):
            col = slice(256 * p, 256 * p + 256)
            skip = skw[:, col] * dy[r, col].astype(F32)
            x_v[r, col] = (skip + dtw[r, col] * dxd[r, col]).astype(BF)
        store(0, c).start()
        return carry

    def settle_from(t, first):
        def one(k, carry):
            settle(t, k)
            return carry

        lax.fori_loop(first, NC, one, 0)

    @pl.when(seq == 0)
    def _():
        s_in[...] = jnp.zeros_like(s_in)

    @pl.when(seq != 0)
    def _():
        for k in range(1, NC):
            from_slab(outf, s_in, rf_send, rf_recv, k).wait_recv()

    repeat(0, NC, finish_y, 4)
    settle_from(1, NC - 2)

    @pl.when(seq == NC - 1)
    def _():
        ds_in[...] = jnp.zeros_like(ds_in)

    @pl.when(seq != NC - 1)
    def _():
        for k in range(1, NC):
            from_slab(outg, ds_in, rg_send, rg_recv, k).wait_recv()

    lax.fori_loop(0, NC // 2, finish_b, 0)
    for p in range(W // 256):
        whole(0, p)
    repeat(0, 2, finish_x, 2)
    settle_from(0, 0)
    repeat(2, NC, finish_x, 2)

    q = qs[...].reshape(L, L)
    px = ps[...].reshape(L, L)
    before = dot(q, (iota0 < iota1).astype(F32), 1, 0, HIGHEST)
    pairs = dot(spread_f, fw[...].reshape(NC, W), 1, 1, HIGHEST)
    boundary = jnp.concatenate([pairs[:, c : c + 1] for c in range(NC)], axis=0)
    d_decay = boundary - before
    d_step = px / step + rate * d_decay
    d_raw = d_step / (1.0 + jnp.exp(-pre))
    for c in range(NC):
        gdt_ref[:, L * c : L * c + L] = d_raw[H * c : H * c + H].astype(BF)

    def over_tokens(v):
        column = jnp.sum(v, axis=1, keepdims=True)
        total = column[0:H]
        for c in range(1, NC):
            total = total + column[H * c : H * c + H]
        return total

    lane16 = lax.broadcasted_iota(jnp.int32, (H, L), 1)
    par[0] = jnp.where(
        lane16 == 0,
        over_tokens(d_decay * decay),
        jnp.where(lane16 == 1, over_tokens(d_raw), skip_sum),
    )

    def share(k):
        return remote(par.at[0], par.at[k], par_send.at[k], par_recv.at[k], slab_dev(k))

    for k in range(1, NC):
        share(k).start()
    repeat(0, NC, finish_gx, 2)
    for k in range(1, NC):
        for t in range(2):
            from_group(t, k).wait_recv()
    outs = [
        pltpu.make_async_copy(gbc.at[0], gb_hbm, gout_sem.at[0]),
        pltpu.make_async_copy(gbc.at[1], gc_hbm, gout_sem.at[1]),
    ]
    for o in outs:
        o.start()
    for k in range(1, NC):
        share(k).wait_recv()
    total = par[0]
    for k in range(1, NC):
        total = total + par[k]
    flat = jnp.transpose(jnp.concatenate([total] * NC, axis=0))
    galog_ref[...] = flat[0:1, 0:H]
    gbias_ref[...] = flat[1:2, 0:H]
    gskip_ref[...] = flat[2:3, 0:H]

    for o in outs:
        o.wait()
    for k in range(NC):
        for t in range(2):
            spread(t, k).wait_send()
            to_sibling(t, k).wait_send()
    for k in range(1, NC):
        for t in range(2):
            forward(t, k, True).wait_send()
            to_owner(t, k).wait_send()

        @pl.when(seq != NC - 1)
        def _():
            to_joiner(sendf, recvf, xf_send, xf_recv, k).wait_send()

        @pl.when(seq != 0)
        def _():
            to_joiner(sendg, recvg, xg_send, xg_recv, k).wait_send()

        @pl.when(slab_at(k) != 0)
        def _():
            back(outf, s_in, rf_send, rf_recv, k).wait_send()

        @pl.when(slab_at(k) != NC - 1)
        def _():
            back(outg, ds_in, rg_send, rg_recv, k).wait_send()

        share(k).wait_send()
    for c in range(NC):
        for a in range(3):
            store(a, c).wait()


def hand_out(*refs):
    ins, outs, held, (in_sem, out_sem) = refs[:9], refs[9:18], refs[18:27], refs[27:]
    blocks = [(a, pl.ds(L * c, L), NC * a + c) for c in range(NC) for a in range(3)]
    blocks += [(a, slice(None), 3 * NC + a - 3) for a in range(3, 9)]
    loads = [pltpu.make_async_copy(ins[a].at[r], held[a].at[r], in_sem.at[s]) for a, r, s in blocks]
    stores = [pltpu.make_async_copy(held[a].at[r], outs[a].at[r], out_sem.at[s]) for a, r, s in blocks]
    for load in loads:
        load.start()
    for load, store in zip(loads, stores):
        load.wait()
        store.start()
    for store in stores:
        store.wait()


def per_device(inner_x, gate_z, dt_raw, b_proj, c_proj, a_log, dt_bias, d_skip, grad_gated):
    tokens = inner_x.shape[0]
    any_space = pl.BlockSpec(memory_space=pl.ANY)
    vmem = pl.BlockSpec(memory_space=pltpu.VMEM)
    smem = pl.BlockSpec(memory_space=pltpu.SMEM)
    sem = pltpu.SemaphoreType.DMA
    big = jax.ShapeDtypeStruct((tokens, W), BF)
    rows = jax.ShapeDtypeStruct((ROWS, GROUPS * STATE), BF)
    head = jax.ShapeDtypeStruct((1, H), F32)
    wide = pltpu.VMEM((tokens, W), BF)
    wide_f = pltpu.VMEM((tokens, W), F32)
    scratch = [
        wide, wide, wide,
        wide, wide, wide, wide,
        wide_f, wide_f, wide_f,
        pltpu.VMEM((2 * H, W), BF),
        pltpu.VMEM((NC, L, 2 * H), BF),
        pltpu.VMEM((NC, L, 2 * H), BF),
        pltpu.VMEM((NC, L, 2 * H), BF),
        pltpu.VMEM((NC, H, L), F32),
        pltpu.VMEM((NC, L, H), F32),
        pltpu.VMEM((NC, 1, W), F32),
        pltpu.VMEM((NC, 1, W), F32),
        pltpu.VMEM((NC + 1, 1, W), F32),
        pltpu.VMEM((1, W), F32),
        pltpu.VMEM((2, tokens, STATE), BF),
        pltpu.VMEM((NC, STATE, W), BF),
        pltpu.VMEM((NC + 1, STATE, W), BF),
        pltpu.VMEM((STATE, W), F32),
        pltpu.VMEM((tokens, W), F32),
        pltpu.VMEM((tokens, W), F32),
        pltpu.VMEM((NC, 2, L, STATE), F32),
        pltpu.VMEM((NC, 2, ROWS, STATE), F32),
        pltpu.VMEM((NC, 2, ROWS, STATE), BF),
        pltpu.VMEM((2, ROWS, GROUPS * STATE), BF),
        pltpu.VMEM((NC, STATE + 16, L), BF),
        pltpu.VMEM((NC, STATE, L), BF),
        pltpu.VMEM((NC, STATE + 16, L), BF),
        pltpu.VMEM((NC, STATE, L), BF),
        pltpu.VMEM((NC, STATE, L), BF),
        pltpu.VMEM((NC, STATE, L), BF),
        pltpu.VMEM((NC, STATE, L), BF),
        pltpu.VMEM((NC, STATE, L), BF),
        pltpu.VMEM((8, W), F32),
        pltpu.VMEM((NC, 1, W), F32),
        pltpu.VMEM((NC, H, L), F32),
        pltpu.VMEM((NC, H, L), F32),
        pltpu.VMEM((NC, H, L), F32),
        sem((3, NC)), sem((3, NC)), sem((2,)),
        sem((2, NC)), sem((2, NC)), sem((2, NC)), sem((2, NC)),
        sem((NC,)), sem((NC,)), sem((NC,)), sem((NC,)),
        sem((NC,)), sem((NC,)), sem((NC,)), sem((NC,)),
        sem((2, NC)), sem((2, NC)), sem((2, NC)), sem((2, NC)), sem((NC,)), sem((NC,)),
        sem((2,)),
    ]
    small = (jax.ShapeDtypeStruct((H, tokens), BF), rows, rows, head, head, head)
    outs = pl.pallas_call(
        kernel,
        out_shape=(big, big, big) + small,
        in_specs=[any_space, any_space, any_space, vmem, any_space, any_space, smem, smem, smem],
        out_specs=(any_space, any_space, any_space, vmem, any_space, any_space, vmem, vmem, vmem),
        scratch_shapes=scratch,
        compiler_params=pltpu.CompilerParams(
            collective_id=0, has_side_effects=True, vmem_limit_bytes=60 * 2**20
        ),
    )(inner_x, gate_z, grad_gated, dt_raw, b_proj, c_proj, a_log, dt_bias, d_skip)
    outs = pl.pallas_call(
        hand_out,
        out_shape=(big, big, big) + small,
        in_specs=[any_space] * 9,
        out_specs=(any_space,) * 9,
        scratch_shapes=[pltpu.VMEM(v.shape, v.dtype) for v in outs]
        + [sem((3 * NC + 6,)), sem((3 * NC + 6,))],
        compiler_params=pltpu.CompilerParams(vmem_limit_bytes=60 * 2**20),
    )(*outs)
    return outs[:6] + tuple(v.reshape(H) for v in outs[6:])


def solution(mesh):
    in_specs = (
        P("seq", "head"),
        P("seq", "head"),
        P("head", "seq"),
        P(("seq", "head"), None),
        P(("seq", "head"), None),
        P("head"),
        P("head"),
        P("head"),
        P("seq", "head"),
    )
    out_specs = (
        P("seq", "head"),
        P("seq", "head"),
        P("seq", "head"),
        P("head", "seq"),
        P(("seq", "head"), None),
        P(("seq", "head"), None),
        P("head"),
        P("head"),
        P("head"),
    )
    return jax.shard_map(
        per_device, mesh=mesh, in_specs=in_specs, out_specs=out_specs, check_vma=False
    )
```
